512 devices in a mesh: image: 32 (over z, x_hi), space: 16 (over x_lo, y, core).
Axes of the slice: x: 4 (x_hi: 2, x_lo: 2; x = x_hi * 2 + x_lo), y: 4, z: 16, core: 2. Of those that a mesh axis runs over, the one named last changes fastest.
Arguments:
- positions: float32 [32, 1024, 3, 128], P('image', 'space'), may hold values from 0 to 1
- velocities: float32 [32, 1024, 3, 128], P('image', 'space'), may hold values from -6 to 6
- counts: int32 [1024], P('space'), may hold values from 64 to 128, as said below
- types: int32 [1024, 128], P('space'), may hold values from 0 to 3
- masses: float32 [4], replicated, may hold values from 1 to 16
Outputs:
- positions_out: float32 [32, 1024, 3, 128], P('image', 'space')
- velocities_out: float32 [32, 1024, 3, 128], P('image', 'space')
The draws below stay inside these ranges and needn't reach their ends.
Inputs may be any that keep to these rules, and one draw needn't show every extreme that they name: `counts`: each cell holds between half of 128 and 128 atoms, and some cell is full.
All inputs are finite; a program needn't handle non-finite values.
Results may differ from the reference program's by a relative error of at most 0.0003.
Values sent between devices are 32-bit elements; how exact they have to be, the bound alone decides.
No kernel may reach another device: no remote copies, remote signals or barrier semaphores. Data moves between devices by JAX's collectives and lax.ppermute only.
A program may use at most 64 MiB of HBM per device.

```python
import math
import jax
import jax.numpy as jnp
from jax import lax

ATOMS_CELL = 128
NTYPES = 4
STEPS = 2
BEADS = 32
CELLS = 1024


def draw_counts(key, part):
    values = jax.random.randint(key, (CELLS,), ATOMS_CELL // 2, ATOMS_CELL + 1)
    return values.at[0].set(ATOMS_CELL).astype(jnp.int32)


def place_ends(result, key, smallest, top_value):
    longest = result.shape.index(max(result.shape))
    spots = []
    for shift in (0, 1):
        where = [jax.random.randint(jax.random.fold_in(key, axis), (), 0, length) for axis, length in enumerate(result.shape)]
        where[longest] = (where[longest] + shift) % result.shape[longest]
        spots.append(tuple(where))
    return result.at[spots[0]].set(smallest).at[spots[1]].set(top_value)


def level_of(stream_key, shape, split, smallest, high):
    factor_of = 1.0
    for dim, shards_of in split:
        heights = jax.random.uniform(jax.random.fold_in(jax.random.fold_in(stream_key, 6), dim), (shards_of,), jnp.float32, smallest / len(split), high / len(split))
        factor_of = factor_of * jnp.repeat(jnp.exp(heights), shape[dim] // shards_of).reshape((-1,) + (1,) * (len(shape) - 1 - dim))
    return factor_of


def normal_values(stream_key, shape, deviation, most, split=(), held_as=jnp.bfloat16):
    gain = level_of(stream_key, shape, split, -0.22, 0.18) if split else 1.0
    values = jax.random.normal(stream_key, shape, jnp.float32) * deviation * gain
    return jnp.minimum(jnp.maximum(values, -most), most).astype(held_as)


def setup_inputs(seed: int = 0) -> dict:
    key_of = jax.random.split(jax.random.key(seed), 6)
    return {
        "positions": jnp.clip(1.0 * jax.random.uniform(key_of[0], (BEADS, CELLS, 3, ATOMS_CELL), jnp.float32) ** level_of(key_of[0], (BEADS, CELLS, 3, ATOMS_CELL), ((0, 32), (1, 16)), -0.2, 0.2), 0.0, 1.0),
        "velocities": normal_values(key_of[1], (BEADS, CELLS, 3, ATOMS_CELL), 1.0, 6.0, ((0, 32), (1, 16)), jnp.float32),
        "counts": draw_counts(jax.random.fold_in(key_of[5], 71), 0),
        "types": place_ends(jax.random.randint(key_of[3], (CELLS, ATOMS_CELL), 0, NTYPES), jax.random.fold_in(key_of[3], 1), 0, NTYPES - 1).astype(jnp.int32),
        "masses": jnp.clip(jnp.exp(jax.random.uniform(key_of[4], (NTYPES,), jnp.float32, math.log(1.0), math.log(16.0))), 1.0, 16.0),
    }


time_step = 1.5
cycle_omega = 6.0
strength = 0.01
width_sq = 0.25

def mode_table(bead_count):
    row_index = lax.broadcasted_iota(jnp.int32, (bead_count, bead_count), 0).astype(jnp.float32)
    col_index = lax.broadcasted_iota(jnp.int32, (bead_count, bead_count), 1).astype(jnp.float32)
    phase_angle = 2.0 * jnp.pi * row_index * col_index / bead_count
    half_count = bead_count // 2
    norm_scale = jnp.sqrt(2.0 / bead_count)
    zero_mode = jnp.ones_like(phase_angle) / jnp.sqrt(float(bead_count))
    middle = jnp.cos(jnp.pi * row_index) / jnp.sqrt(float(bead_count))
    return jnp.where(col_index == 0, zero_mode, jnp.where(col_index < half_count, norm_scale * jnp.cos(phase_angle), jnp.where(col_index == half_count, middle, norm_scale * jnp.sin(phase_angle))))

def mode_factors(bead_count):
    mode_index = lax.iota(jnp.int32, bead_count).astype(jnp.float32)
    mode_omega = 2.0 * cycle_omega * jnp.sin(jnp.pi * mode_index / bead_count)
    mode_angle = mode_omega * time_step
    cosine = jnp.cos(mode_angle)
    safe_omega = jnp.where(mode_index == 0, 1.0, mode_omega)
    to_velocity = jnp.where(mode_index == 0, 0.0, -mode_omega * jnp.sin(mode_angle))
    to_position = jnp.where(mode_index == 0, time_step, jnp.sin(mode_angle) / safe_omega)
    return (cosine, to_velocity, to_position)

def free_cycle(positions, velocities):
    bead_count = positions.shape[0]
    transform = mode_table(bead_count)
    cosine, to_velocity, to_position = mode_factors(bead_count)
    cosine = cosine[:, None, None, None]
    to_velocity = to_velocity[:, None, None, None]
    to_position = to_position[:, None, None, None]
    mode_pos = jnp.einsum('jk,jcxa->kcxa', transform, positions, precision=lax.Precision.HIGHEST)
    mode_vel = jnp.einsum('jk,jcxa->kcxa', transform, velocities, precision=lax.Precision.HIGHEST)
    next_vel = cosine * mode_vel + to_velocity * mode_pos
    next_pos = to_position * mode_vel + cosine * mode_pos
    new_pos = jnp.einsum('jk,kcxa->jcxa', transform, next_pos, precision=lax.Precision.HIGHEST)
    new_vel = jnp.einsum('jk,kcxa->jcxa', transform, next_vel, precision=lax.Precision.HIGHEST)
    return (new_pos, new_vel)

def cell_force(own_pos, own_mask, near_pos, near_mask):
    offset = (lax.iota(jnp.int32, 3) - 1).astype(jnp.float32)
    diff_x = own_pos[:, None, 0, :, None] - near_pos[:, :, 0, None, :] - offset[None, :, None, None]
    diff_y = own_pos[:, None, 1, :, None] - near_pos[:, :, 1, None, :]
    diff_z = own_pos[:, None, 2, :, None] - near_pos[:, :, 2, None, :]
    weight = strength / width_sq * jnp.exp(-(diff_x * diff_x + diff_y * diff_y + diff_z * diff_z) / (2.0 * width_sq))
    weight = weight * near_mask[:, :, None, :]
    force_x = lax.optimization_barrier(jnp.sum(weight * diff_x, axis=(1, 3)))
    force_y = lax.optimization_barrier(jnp.sum(weight * diff_y, axis=(1, 3)))
    force_z = lax.optimization_barrier(jnp.sum(weight * diff_z, axis=(1, 3)))
    return jnp.stack([force_x, force_y, force_z], axis=1) * own_mask[:, None, :]

def bead_forces(bead_field, occupied):
    near_pos = jnp.stack([jnp.roll(bead_field, 1, 0), bead_field, jnp.roll(bead_field, -1, 0)], axis=1)
    near_mask = jnp.stack([jnp.roll(occupied, 1, 0), occupied, jnp.roll(occupied, -1, 0)], axis=1)
    cell_count = bead_field.shape[0]
    block_cells = 8

    def block_force(block_index):
        block_start = (block_index * block_cells).astype(jnp.int32)
        return cell_force(lax.dynamic_slice_in_dim(bead_field, block_start, block_cells, 0), lax.dynamic_slice_in_dim(occupied, block_start, block_cells, 0), lax.dynamic_slice_in_dim(near_pos, block_start, block_cells, 0), lax.dynamic_slice_in_dim(near_mask, block_start, block_cells, 0))
    blocked = lax.map(block_force, jnp.arange(cell_count // block_cells, dtype=jnp.int32))
    return blocked.reshape(bead_field.shape)

def all_forces(positions, occupied):
    return lax.map(lambda bead_field: bead_forces(bead_field, occupied), positions)

def reference(positions, velocities, counts, types, masses):
    slot_index = lax.broadcasted_iota(jnp.int32, types.shape, 1)
    occupied = (slot_index < counts[:, None]).astype(jnp.float32)
    inverse_mass = 1.0 / masses[types]
    kick_scale = 0.5 * time_step * inverse_mass[None, :, None, :]
    forces_now = all_forces(positions, occupied)
    for step_index in range(STEPS):
        velocities = velocities + kick_scale * forces_now
        positions, velocities = free_cycle(positions, velocities)
        forces_now = all_forces(positions, occupied)
        velocities = velocities + kick_scale * forces_now
    return (positions, velocities)
```

```python
import math

import jax
import jax.numpy as jnp
import numpy as np
from jax import lax
from jax.experimental import pallas as pl
from jax.experimental.pallas import tpu as pltpu
from jax.sharding import PartitionSpec as P

STEPS = 2

time_step = 1.5
cycle_omega = 6.0
strength = 0.01
width_sq = 0.25

F32 = jnp.float32
BF16 = jnp.bfloat16
LANES = 128
ROWS = 24
SPAN = 12
ALPHA = math.sqrt(math.log2(math.e) / width_sq)
GAIN = strength / width_sq / ALPHA
FAR = 1e12


def cycle_matrix(count):
    j = np.arange(count, dtype=np.float64)[:, None]
    k = np.arange(count, dtype=np.float64)[None, :]
    half = count // 2
    phase = 2.0 * np.pi * j * k / count
    table = np.where(
        k < half, np.sqrt(2.0 / count) * np.cos(phase), np.sqrt(2.0 / count) * np.sin(phase)
    )
    table = np.where(k == 0, 1.0 / np.sqrt(count), table)
    table = np.where(k == half, np.cos(np.pi * j) / np.sqrt(count), table)
    omega = 2.0 * cycle_omega * np.sin(np.pi * k[0] / count)
    angle = omega * time_step
    to_position = np.where(k[0] == 0, time_step, np.sin(angle) / np.where(k[0] == 0, 1.0, omega))
    same = (table * np.cos(angle)) @ table.T
    from_velocity = (table * to_position) @ table.T
    from_position = (table * (-omega * np.sin(angle))) @ table.T
    return np.block([[same, from_velocity], [from_position, same]]).astype(np.float32)


def split3(value):
    high = value.astype(BF16).astype(F32)
    rest = value - high
    mid = rest.astype(BF16).astype(F32)
    low = (rest - mid).astype(BF16).astype(F32)
    return high, mid, low


def put_tables(planes, occupied, tables, start, stride=1):
    left, right, moved = tables
    count = planes[0].shape[0]
    one = jnp.ones_like(planes[0])

    def put(ref, row, value):
        ref[pl.ds(start * ROWS + row, count, stride=stride * ROWS), :] = value

    def norm(parts):
        total = parts[0] * parts[0] + parts[1] * parts[1] + parts[2] * parts[2]
        return split3(-0.5 * total - FAR * (1.0 - occupied))

    scaled = [ALPHA * plane for plane in planes]
    pieces = [split3(part) for part in scaled]
    norms = norm(scaled)
    for axis in range(3):
        high, mid, low = pieces[axis]
        for row, value in ((0, high), (4, mid), (8, high), (12, low), (16, high), (20, mid)):
            put(left, row + axis, value)
        for row, value in ((0, high), (4, high), (8, mid), (12, high), (16, low), (20, mid)):
            put(right, row + axis, value)
            if axis:
                put(moved, row + axis, value)
    for piece in range(3):
        put(left, 8 * piece + 3, norms[piece])
        put(left, 8 * piece + 7, one)
        put(right, 8 * piece + 3, one)
        put(right, 8 * piece + 7, norms[piece])
        put(moved, 8 * piece + 3, one)
    ahead = ALPHA * (planes[0] + 1.0)
    high, mid, low = split3(ahead)
    for row, value in ((0, high), (4, high), (8, mid), (12, high), (16, low), (20, mid)):
        put(moved, row, value)
    norms = norm([ahead, scaled[1], scaled[2]])
    for piece in range(3):
        put(moved, 8 * piece + 7, norms[piece])


def fold(sums):
    return sums[0:8], sums[0:8] + sums[8:16] + sums[16:24]


def pair_sums(tables, own, near):
    left, right, moved = tables
    pad = jnp.zeros((8, LANES), F32)

    def rows(ref, cell):
        return ref[pl.ds(pl.multiple_of(cell * ROWS, 8), ROWS), :]

    table = rows(right, own)
    place = table[0:8] + table[8:16] + table[16:24]
    left_rows = jnp.concatenate([rows(left, own), pad], axis=0).astype(BF16)
    own_rows = jnp.concatenate([table, pad], axis=0).astype(BF16)
    near_rows = jnp.concatenate([rows(moved, near), pad], axis=0).astype(BF16)
    both = jnp.concatenate([own_rows, near_rows], axis=1)
    exponent = lax.dot_general(
        left_rows, both, (((0,), (0,)), ((), ())), preferred_element_type=F32
    )
    weight = jnp.exp2(exponent).astype(BF16)
    to_own = lax.dot_general(
        both, weight, (((1,), (1,)), ((), ())), preferred_element_type=F32
    )
    to_near = lax.dot_general(
        own_rows, weight[:, LANES:], (((1,), (0,)), ((), ())), preferred_element_type=F32
    )
    return place, fold(to_own), fold(to_near)


def force_of(place, sums, carry):
    shift = jnp.where(lax.broadcasted_iota(jnp.int32, (8, LANES), 0) == 0, ALPHA, 0.0)
    from_right = place * sums[0][3:4] - sums[1]
    from_left = (place + shift) * carry[0][3:4] - carry[1]
    return GAIN * (from_right + from_left)


def chain_forces(tables, count, emit):
    zero = jnp.zeros((8, LANES), F32)
    unroll = next(u for u in (5, 3, 1) if (count - 1) % u == 0)

    def body(step, carry):
        for part in range(unroll):
            cell = step * unroll + part
            place, sums, onward = pair_sums(tables, cell, cell + 1)
            emit(cell, force_of(place, sums, carry))
            carry = onward
        return carry

    lax.fori_loop(0, (count - 1) // unroll, body, (zero, zero))


def scratch(rows):
    return pltpu.VMEM((rows, LANES), F32)


VMEM = pl.BlockSpec(memory_space=pltpu.VMEM)
PARAMS = pltpu.CompilerParams(vmem_limit_bytes=48 * 1024 * 1024)


def edge_kernel(cells, pos_ref, vel_ref, occ_ref, kick_ref, out_ref):
    for axis in range(3):
        out_ref[axis : axis + 1, :] = pos_ref[axis, cells - 2 : cells - 1, :]
        out_ref[3 + axis : 4 + axis, :] = pos_ref[axis, cells - 1 : cells, :]
        out_ref[6 + axis : 7 + axis, :] = vel_ref[axis, cells - 1 : cells, :]
    out_ref[9:11, :] = occ_ref[cells - 2 : cells, :]
    out_ref[11:12, :] = kick_ref[cells - 1 : cells, :]
    out_ref[12:16, :] = jnp.zeros((4, LANES), F32)


def first_kernel(
    cells, edge_ref, pos_ref, vel_ref, occ_ref, kick_ref, send_ref,
    place, speed, occ_all, left, right, moved,
):
    half = cells // 4
    place[0:3, :] = edge_ref[0:3, :]
    place[8:11, :] = edge_ref[3:6, :]
    speed[8:11, :] = edge_ref[6:9, :]
    place[11:12, :] = edge_ref[11:12, :]
    for axis in range(3):
        place[pl.ds(2 * 8 + axis, cells, stride=8), :] = pos_ref[axis]
        speed[pl.ds(2 * 8 + axis, cells, stride=8), :] = vel_ref[axis]
    place[pl.ds(2 * 8 + 3, cells, stride=8), :] = kick_ref[...]
    occ_all[0:2, :] = edge_ref[9:11, :]
    occ_all[2 : cells + 2, :] = occ_ref[...]
    tables = (left, right, moved)
    count = cells + 8
    planes = [place[pl.ds(axis, count, stride=8), :] for axis in range(3)]
    put_tables(planes, occ_all[...], tables, 0)

    def emit(slot, force):
        rows = pl.ds(pl.multiple_of(slot * 8, 8), 8)
        kick = place[rows, :][3:4]
        speed[rows, :] = speed[rows, :] + kick * force

    chain_forces(tables, cells + 2, emit)
    for kind, source in enumerate((place, speed)):
        for axis in range(3):
            for parity in range(2):
                row = (kind * 3 + axis) * 2 + parity
                for part in range(2):
                    first = (part * 2 * half + 1 + parity) * 8 + axis
                    send_ref[pl.ds(part * SPAN + row, half, stride=2 * SPAN), :] = source[
                        pl.ds(first, half, stride=16), :
                    ]


def cycle(matrix_ref, blocks):
    return jnp.dot(
        matrix_ref[...],
        jnp.concatenate(blocks, axis=1),
        precision=lax.Precision.HIGHEST,
        preferred_element_type=F32,
    )


def turn_kernel(images, matrix_ref, got_ref, low_ref, high_ref, vel_ref):
    blocks = []
    for parity in range(2):
        for axis in range(3):
            parts = [
                got_ref[pl.ds((kind * 3 + axis) * 2 + parity, images, stride=SPAN), :]
                for kind in range(2)
            ]
            blocks.append(jnp.concatenate(parts, axis=0))
    ahead = cycle(matrix_ref, blocks)
    for parity, out_ref in enumerate((low_ref, high_ref)):
        for axis in range(3):
            index = parity * 3 + axis
            lanes = slice(index * LANES, (index + 1) * LANES)
            out_ref[axis * images : (axis + 1) * images, :] = ahead[:images, lanes]
            vel_ref[index * images : (index + 1) * images, :] = ahead[images:, lanes]


def middle_kernel(
    images, matrix_ref, info_ref, before_ref, low_ref, high_ref, after_ref, vel_ref, send_ref,
    forces, left, right, moved,
):
    tables = (left, right, moved)
    for slot, ref in enumerate((before_ref, low_ref, high_ref, after_ref)):
        planes = [ref[axis * images : (axis + 1) * images, :] for axis in range(3)]
        occupied = jnp.broadcast_to(info_ref[slot : slot + 1, :], (images, LANES))
        put_tables(planes, occupied, tables, slot, stride=4)

    def body(image, _):
        first = image * 4
        place, sums, carry = pair_sums(tables, first, first + 1)
        for parity in range(2):
            place, sums, onward = pair_sums(tables, first + 1 + parity, first + 2 + parity)
            rows = pl.ds(pl.multiple_of((image * 2 + parity) * 8, 8), 8)
            forces[rows, :] = force_of(place, sums, carry)
            carry = onward
        return 0

    def two(step, _):
        body(step * 2, 0)
        body(step * 2 + 1, 0)
        return 0

    lax.fori_loop(0, images // 2, two, 0)
    blocks = []
    for parity, ref in enumerate((low_ref, high_ref)):
        kick = 2.0 * info_ref[4 + parity : 5 + parity, :]
        for axis in range(3):
            index = parity * 3 + axis
            force = forces[pl.ds(parity * 8 + axis, images, stride=16), :]
            speed = vel_ref[index * images : (index + 1) * images, :] + kick * force
            blocks.append(
                jnp.concatenate([ref[axis * images : (axis + 1) * images, :], speed], axis=0)
            )
    ahead = cycle(matrix_ref, blocks)
    for parity in range(2):
        for axis in range(3):
            index = parity * 3 + axis
            lanes = slice(index * LANES, (index + 1) * LANES)
            for kind in range(2):
                row = (kind * 3 + axis) * 2 + parity
                send_ref[pl.ds(row, images, stride=SPAN), :] = ahead[
                    kind * images : (kind + 1) * images, lanes
                ]


def last_kernel(
    cells, got_ref, edge_ref, first_ref, occ_ref, kick_ref, pos_ref, vel_ref,
    place, speed, occ_all, left, right, moved,
):
    half = cells // 4
    for kind, target in enumerate((place, speed)):
        for axis in range(3):
            for parity in range(2):
                row = (kind * 3 + axis) * 2 + parity
                for part in range(2):
                    first = (part * 2 * half + parity) * 8 + axis
                    target[pl.ds(first, half, stride=16), :] = got_ref[
                        pl.ds(part * SPAN + row, half, stride=2 * SPAN), :
                    ]
                if kind == 0 or parity == 0:
                    slot = (cells + parity) * 8 + axis
                    target[slot : slot + 1, :] = edge_ref[row : row + 1, :]
    place[pl.ds(8 + 3, cells, stride=8), :] = kick_ref[...]
    occ_all[0:1, :] = first_ref[10:11, :]
    occ_all[1 : cells + 1, :] = occ_ref[...]
    occ_all[cells + 1 : cells + 2, :] = edge_ref[12:13, :]
    tables = (left, right, moved)
    count = cells + 8
    planes = [place[pl.ds(axis, count, stride=8), :] for axis in range(3)]
    put_tables(planes, occ_all[...], tables, 0)

    def emit(slot, force):
        rows = pl.ds(pl.multiple_of(slot * 8, 8), 8)
        kick = place[rows, :][3:4]
        speed[rows, :] = speed[rows, :] + kick * force

    chain_forces(tables, cells + 2, emit)
    for axis in range(3):
        pos_ref[axis] = place[pl.ds(8 + axis, cells, stride=8), :]
        vel_ref[axis] = speed[pl.ds(8 + axis, cells, stride=8), :]


def local(positions, velocities, counts, types, masses):
    images = lax.axis_size("image")
    slabs = lax.axis_size("space")
    cells = positions.shape[1]
    rows = cells + 8
    place_of = lambda block: 2 * (block % (images // 2)) + block // (images // 2)

    def device(block):
        block %= images * slabs
        slab, inside = divmod(block, images)
        return place_of(inside) * slabs + slab

    def shift(array, distance):
        pairs = [(device(b), device(b + distance)) for b in range(images * slabs)]
        return lax.ppermute(array, ("image", "space"), pairs)

    def slab_shift(array, distance):
        pairs = [(s, (s + distance) % slabs) for s in range(slabs)]
        return lax.ppermute(array, "space", pairs)

    def transpose(array):
        blocks = array.reshape(images, SPAN // 4, 4, LANES)
        blocks = lax.all_to_all(blocks, "image", split_axis=0, concat_axis=0, tiled=True)
        return blocks.reshape(array.shape)

    def call(kernel, outs, scratches, *args):
        return pl.pallas_call(
            kernel,
            out_shape=outs,
            in_specs=[VMEM] * len(args),
            out_specs=jax.tree.map(lambda _: VMEM, outs),
            scratch_shapes=scratches,
            compiler_params=PARAMS,
        )(*args)

    def shaped(*shape):
        return jax.ShapeDtypeStruct(shape, F32)

    slot_index = lax.broadcasted_iota(jnp.int32, types.shape, 1)
    occupied = (slot_index < counts[:, None]).astype(F32)
    type_index = lax.broadcasted_iota(jnp.int32, (masses.shape[0],) + types.shape, 0)
    chosen = jnp.sum(jnp.where(types[None] == type_index, masses[:, None, None], 0.0), axis=0)
    kick = 0.5 * time_step * (1.0 / chosen)
    matrix = jnp.asarray(cycle_matrix(images))
    group = lax.axis_index("image")
    block = (group % 2) * (images // 2) + group // 2

    pos = positions[0].transpose(1, 0, 2)
    vel = velocities[0].transpose(1, 0, 2)
    cell_tables = [scratch(rows * ROWS)] * 3
    edge = call(lambda *r: edge_kernel(cells, *r), shaped(16, LANES), [], pos, vel, occupied, kick)
    edge = slab_shift(edge, 1)
    send = call(
        lambda *r: first_kernel(cells, *r),
        shaped(images * SPAN, LANES),
        [scratch(rows * 8), scratch(rows * 8), scratch(rows)] + cell_tables,
        edge, pos, vel, occupied, kick,
    )
    got = transpose(send)
    low, high, speed = call(
        lambda *r: turn_kernel(images, *r),
        (shaped(3 * images, LANES), shaped(3 * images, LANES), shaped(6 * images, LANES)),
        [],
        matrix, got,
    )
    before = shift(high, 1)
    after = shift(low, -1)
    occ_wide = jnp.concatenate([edge[9:11], occupied], axis=0)
    kick_wide = jnp.concatenate([edge[11:12], kick], axis=0)
    info = jnp.concatenate(
        [
            lax.dynamic_slice_in_dim(occ_wide, 2 * block, 4, 0),
            lax.dynamic_slice_in_dim(kick_wide, 2 * block, 2, 0),
            jnp.zeros((2, LANES), F32),
        ],
        axis=0,
    )
    send = call(
        lambda *r: middle_kernel(images, *r),
        shaped(images * SPAN, LANES),
        [scratch(2 * images * 8)] + [scratch(4 * images * ROWS)] * 3,
        matrix, info, before, low, high, after, speed,
    )
    got = transpose(send)
    message = jnp.concatenate([got[0:SPAN], occupied[0:1], jnp.zeros((3, LANES), F32)], axis=0)
    message = slab_shift(message, -1)
    pos, vel = call(
        lambda *r: last_kernel(cells, *r),
        (shaped(*pos.shape), shaped(*vel.shape)),
        [scratch(rows * 8), scratch(rows * 8), scratch(rows)] + cell_tables,
        got, message, edge, occupied, kick,
    )
    return pos.transpose(1, 0, 2)[None], vel.transpose(1, 0, 2)[None]


def solution(mesh):
    return jax.shard_map(
        local,
        mesh=mesh,
        in_specs=(
            P("image", "space", None, None),
            P("image", "space", None, None),
            P("space"),
            P("space", None),
            P(),
        ),
        out_specs=(P("image", "space", None, None), P("image", "space", None, None)),
        check_vma=False,
    )
```

```python
import math

import jax
import jax.numpy as jnp
import numpy as np
from jax import lax
from jax.experimental import pallas as pl
from jax.experimental.pallas import tpu as pltpu
from jax.sharding import PartitionSpec as P

STEPS = 2

time_step = 1.5
cycle_omega = 6.0
strength = 0.01
width_sq = 0.25

F32 = jnp.float32
BF16 = jnp.bfloat16
LANES = 128
ROWS = 24
SPAN = 12
WIDE = 24
ALPHA = math.sqrt(math.log2(math.e) / width_sq)
GAIN = strength / width_sq / ALPHA
FAR = 1e12


def cycle_matrix(count):
    j = np.arange(count, dtype=np.float64)[:, None]
    k = np.arange(count, dtype=np.float64)[None, :]
    half = count // 2
    phase = 2.0 * np.pi * j * k / count
    table = np.where(
        k < half, np.sqrt(2.0 / count) * np.cos(phase), np.sqrt(2.0 / count) * np.sin(phase)
    )
    table = np.where(k == 0, 1.0 / np.sqrt(count), table)
    table = np.where(k == half, np.cos(np.pi * j) / np.sqrt(count), table)
    omega = 2.0 * cycle_omega * np.sin(np.pi * k[0] / count)
    angle = omega * time_step
    to_position = np.where(k[0] == 0, time_step, np.sin(angle) / np.where(k[0] == 0, 1.0, omega))
    same = (table * np.cos(angle)) @ table.T
    from_velocity = (table * to_position) @ table.T
    from_position = (table * (-omega * np.sin(angle))) @ table.T
    return np.block([[same, from_velocity], [from_position, same]]).astype(np.float32)


def split3(value):
    high = value.astype(BF16).astype(F32)
    rest = value - high
    mid = rest.astype(BF16).astype(F32)
    low = (rest - mid).astype(BF16).astype(F32)
    return high, mid, low


def put_tables(planes, occupied, tables, start, stride=1):
    left, right, moved = tables
    count = planes[0].shape[0]
    one = jnp.ones_like(planes[0])

    def put(ref, row, value):
        ref[pl.ds(start * ROWS + row, count, stride=stride * ROWS), :] = value

    def norm(parts):
        total = parts[0] * parts[0] + parts[1] * parts[1] + parts[2] * parts[2]
        return split3(-0.5 * total - FAR * (1.0 - occupied))

    scaled = [ALPHA * plane for plane in planes]
    pieces = [split3(part) for part in scaled]
    norms = norm(scaled)
    for axis in range(3):
        high, mid, low = pieces[axis]
        for row, value in ((0, high), (4, mid), (8, high), (12, low), (16, high), (20, mid)):
            put(left, row + axis, value)
        for row, value in ((0, high), (4, high), (8, mid), (12, high), (16, low), (20, mid)):
            put(right, row + axis, value)
            if axis:
                put(moved, row + axis, value)
    for piece in range(3):
        put(left, 8 * piece + 3, norms[piece])
        put(left, 8 * piece + 7, one)
        put(right, 8 * piece + 3, one)
        put(right, 8 * piece + 7, norms[piece])
        put(moved, 8 * piece + 3, one)
    ahead = ALPHA * (planes[0] + 1.0)
    high, mid, low = split3(ahead)
    for row, value in ((0, high), (4, high), (8, mid), (12, high), (16, low), (20, mid)):
        put(moved, row, value)
    norms = norm([ahead, scaled[1], scaled[2]])
    for piece in range(3):
        put(moved, 8 * piece + 7, norms[piece])


def table_rows(ref, cell):
    return ref[cell * ROWS : (cell + 1) * ROWS, :]


def factor(table):
    pad = jnp.zeros((8, LANES), F32)
    return jnp.concatenate([table, pad], axis=0).astype(BF16)


def put_weights(tables, weights, index, own, near, full):
    left, right, moved = tables
    others = factor(table_rows(moved, near))
    if full:
        others = jnp.concatenate([factor(table_rows(right, own)), others], axis=1)
    exponent = lax.dot_general(
        factor(table_rows(left, own)),
        others,
        (((0,), (0,)), ((), ())),
        preferred_element_type=F32,
    )
    start = 0 if full else LANES
    weights[index * LANES : (index + 1) * LANES, start:] = jnp.exp2(exponent).astype(BF16)


def fold(sums):
    return sums[0:8], sums[0:8] + sums[8:16] + sums[16:24]


def own_sums(tables, weights, index, own, near):
    both = jnp.concatenate(
        [factor(table_rows(tables[1], own)), factor(table_rows(tables[2], near))], axis=1
    )
    weight = weights[index * LANES : (index + 1) * LANES, :]
    return fold(
        lax.dot_general(both, weight, (((1,), (1,)), ((), ())), preferred_element_type=F32)
    )


def next_sums(tables, weights, index, own):
    weight = weights[index * LANES : (index + 1) * LANES, LANES:]
    return fold(
        lax.dot_general(
            factor(table_rows(tables[1], own)),
            weight,
            (((1,), (0,)), ((), ())),
            preferred_element_type=F32,
        )
    )


def force_of(tables, own, sums, carry):
    table = table_rows(tables[1], own)
    place = table[0:8] + table[8:16] + table[16:24]
    shift = jnp.where(lax.broadcasted_iota(jnp.int32, (8, LANES), 0) == 0, ALPHA, 0.0)
    from_right = place * sums[0][3:4] - sums[1]
    from_left = (place + shift) * carry[0][3:4] - carry[1]
    return GAIN * (from_right + from_left)


def chain_forces(tables, weights, chains, emit, group):
    steps = [
        (own, own > first, own + 1 < last)
        for first, last in chains
        for own in range(first, last)
    ]
    carry = None
    for start in range(0, len(steps), group):
        part = list(enumerate(steps))[start : start + group]
        for index, (own, inner, _) in part:
            put_weights(tables, weights, index, own, own + 1, inner)
        for index, (own, inner, more) in part:
            if inner:
                sums = own_sums(tables, weights, index, own, own + 1)
                emit(own, force_of(tables, own, sums, carry))
            carry = next_sums(tables, weights, index, own) if more else None


def scratch(rows):
    return pltpu.VMEM((rows, LANES), F32)


VMEM = pl.BlockSpec(memory_space=pltpu.VMEM)
PARAMS = pltpu.CompilerParams(vmem_limit_bytes=48 * 1024 * 1024)


def edge_kernel(cells, pos_ref, vel_ref, occ_ref, kick_ref, out_ref):
    for axis in range(3):
        out_ref[axis * 4 : axis * 4 + 4, :] = pos_ref[axis, cells - 4 : cells, :]
        out_ref[12 + axis * 3 : 15 + axis * 3, :] = vel_ref[axis, cells - 3 : cells, :]
    out_ref[21:24, :] = kick_ref[cells - 3 : cells, :]
    out_ref[24:28, :] = occ_ref[cells - 4 : cells, :]
    out_ref[28:32, :] = jnp.zeros((4, LANES), F32)


def first_kernel(
    cells, edge_ref, pos_ref, vel_ref, occ_ref, kick_ref, send_ref,
    place, speed, occ_all, weights, left, right, moved,
):
    half = cells // 4
    for axis in range(3):
        place[pl.ds(axis, 4, stride=8), :] = edge_ref[axis * 4 : axis * 4 + 4, :]
        place[pl.ds(4 * 8 + axis, cells, stride=8), :] = pos_ref[axis]
        speed[pl.ds(8 + axis, 3, stride=8), :] = edge_ref[12 + axis * 3 : 15 + axis * 3, :]
        speed[pl.ds(4 * 8 + axis, cells, stride=8), :] = vel_ref[axis]
    place[pl.ds(8 + 3, 3, stride=8), :] = edge_ref[21:24, :]
    place[pl.ds(4 * 8 + 3, cells, stride=8), :] = kick_ref[...]
    occ_all[0:4, :] = edge_ref[24:28, :]
    occ_all[4 : cells + 4, :] = occ_ref[...]
    tables = (left, right, moved)
    count = cells + 8
    planes = [place[pl.ds(axis, count, stride=8), :] for axis in range(3)]
    put_tables(planes, occ_all[...], tables, 0)

    def emit(slot, force):
        rows = slice(slot * 8, slot * 8 + 8)
        speed[rows, :] = speed[rows, :] + place[rows, :][3:4] * force

    chain_forces(tables, weights, [(0, cells + 3)], emit, 13)
    for kind, source in enumerate((place, speed)):
        for axis in range(3):
            for near in range(4):
                row = (kind * 3 + axis) * 4 + near
                for part in range(2):
                    first = (part * 2 * half + 1 + near) * 8 + axis
                    send_ref[pl.ds(part * WIDE + row, half, stride=2 * WIDE), :] = source[
                        pl.ds(first, half, stride=16), :
                    ]


def cycle(matrix, blocks):
    return jnp.dot(
        matrix,
        jnp.concatenate(blocks, axis=1),
        precision=lax.Precision.HIGHEST,
        preferred_element_type=F32,
    )


def lanes_of(array, index):
    return array[:, index * LANES : (index + 1) * LANES]


def middle_kernel(
    images, matrix_ref, info_ref, got_ref, send_ref, forces, weights, left, right, moved
):
    tables = (left, right, moved)

    def blocks_of(slots):
        return [
            jnp.concatenate(
                [
                    got_ref[pl.ds((kind * 3 + axis) * 4 + slot, images, stride=WIDE), :]
                    for kind in range(2)
                ],
                axis=0,
            )
            for slot in slots
            for axis in range(3)
        ]

    inner = cycle(matrix_ref[...], blocks_of((1, 2)))
    outer = cycle(matrix_ref[:images, :], blocks_of((0, 3)))
    for slot in range(4):
        source, first = ((outer, 0), (inner, 0), (inner, 3), (outer, 3))[slot]
        planes = [lanes_of(source, first + axis)[:images] for axis in range(3)]
        occupied = jnp.broadcast_to(info_ref[slot : slot + 1, :], (images, LANES))
        put_tables(planes, occupied, tables, slot, stride=4)

    def emit(cell, force):
        row = (cell // 4 * 2 + cell % 4 - 1) * 8
        forces[row : row + 8, :] = force

    chains = [(4 * image, 4 * image + 3) for image in range(images)]
    chain_forces(tables, weights, chains, emit, 12)
    blocks = []
    for parity in range(2):
        kick = 2.0 * info_ref[4 + parity : 5 + parity, :]
        for axis in range(3):
            now = lanes_of(inner, parity * 3 + axis)
            force = forces[pl.ds(parity * 8 + axis, images, stride=16), :]
            blocks.append(jnp.concatenate([now[:images], now[images:] + kick * force], axis=0))
    ahead = cycle(matrix_ref[...], blocks)
    for parity in range(2):
        for axis in range(3):
            after = lanes_of(ahead, parity * 3 + axis)
            for kind in range(2):
                row = (kind * 3 + axis) * 2 + parity
                send_ref[pl.ds(row, images, stride=SPAN), :] = after[
                    kind * images : (kind + 1) * images
                ]


def last_kernel(
    cells, got_ref, edge_ref, first_ref, occ_ref, kick_ref, pos_ref, vel_ref,
    place, speed, occ_all, weights, left, right, moved,
):
    half = cells // 4
    for kind, target in enumerate((place, speed)):
        for axis in range(3):
            for parity in range(2):
                row = (kind * 3 + axis) * 2 + parity
                for part in range(2):
                    first = (part * 2 * half + parity) * 8 + axis
                    target[pl.ds(first, half, stride=16), :] = got_ref[
                        pl.ds(part * SPAN + row, half, stride=2 * SPAN), :
                    ]
                slot = (cells + parity) * 8 + axis
                target[slot : slot + 1, :] = edge_ref[row : row + 1, :]
    for axis in range(3):
        slot = (cells + 2) * 8 + axis
        place[slot : slot + 1, :] = edge_ref[12 + axis : 13 + axis, :]
    place[pl.ds(2 * 8 + 3, cells, stride=8), :] = kick_ref[...]
    occ_all[0:2, :] = first_ref[26:28, :]
    occ_all[2 : cells + 2, :] = occ_ref[...]
    occ_all[cells + 2 : cells + 3, :] = edge_ref[15:16, :]
    tables = (left, right, moved)
    count = cells + 8
    planes = [place[pl.ds(axis, count, stride=8), :] for axis in range(3)]
    put_tables(planes, occ_all[...], tables, 0)

    def emit(slot, force):
        rows = slice(slot * 8, slot * 8 + 8)
        speed[rows, :] = speed[rows, :] + place[rows, :][3:4] * force

    chain_forces(tables, weights, [(1, cells + 2)], emit, 13)
    for axis in range(3):
        pos_ref[axis] = place[pl.ds(2 * 8 + axis, cells, stride=8), :]
        vel_ref[axis] = speed[pl.ds(2 * 8 + axis, cells, stride=8), :]


def local(positions, velocities, counts, types, masses):
    images = lax.axis_size("image")
    slabs = lax.axis_size("space")
    cells = positions.shape[1]
    rows = cells + 8

    def slab_shift(array, distance):
        pairs = [(s, (s + distance) % slabs) for s in range(slabs)]
        return lax.ppermute(array, "space", pairs)

    def transpose(array):
        blocks = array.reshape(images, array.shape[0] // images // 4, 4, LANES)
        blocks = lax.all_to_all(blocks, "image", split_axis=0, concat_axis=0, tiled=True)
        return blocks.reshape(array.shape)

    def call(kernel, outs, scratches, *args):
        return pl.pallas_call(
            kernel,
            out_shape=outs,
            in_specs=[VMEM] * len(args),
            out_specs=jax.tree.map(lambda _: VMEM, outs),
            scratch_shapes=scratches,
            compiler_params=PARAMS,
        )(*args)

    def shaped(*shape):
        return jax.ShapeDtypeStruct(shape, F32)

    def weight_scratch(steps):
        return pltpu.VMEM((steps * LANES, 2 * LANES), BF16)

    slot_index = lax.broadcasted_iota(jnp.int32, types.shape, 1)
    occupied = (slot_index < counts[:, None]).astype(F32)
    type_index = lax.broadcasted_iota(jnp.int32, (masses.shape[0],) + types.shape, 0)
    chosen = jnp.sum(jnp.where(types[None] == type_index, masses[:, None, None], 0.0), axis=0)
    kick = 0.5 * time_step * (1.0 / chosen)
    matrix = jnp.asarray(cycle_matrix(images))
    group = lax.axis_index("image")
    block = (group % 2) * (images // 2) + group // 2

    pos = positions[0].transpose(1, 0, 2)
    vel = velocities[0].transpose(1, 0, 2)
    slab_scratch = [scratch(rows * 8), scratch(rows * 8), scratch(rows), weight_scratch(rows)]
    slab_scratch += [scratch(rows * ROWS)] * 3
    edge = call(lambda *r: edge_kernel(cells, *r), shaped(32, LANES), [], pos, vel, occupied, kick)
    edge = slab_shift(edge, 1)
    send = call(
        lambda *r: first_kernel(cells, *r),
        shaped(images * WIDE, LANES),
        slab_scratch,
        edge, pos, vel, occupied, kick,
    )
    got = transpose(send)
    occ_wide = jnp.concatenate([edge[24:28], occupied], axis=0)
    kick_wide = jnp.concatenate([edge[21:24], kick], axis=0)
    info = jnp.concatenate(
        [
            lax.dynamic_slice_in_dim(occ_wide, 2 * block + 1, 4, 0),
            lax.dynamic_slice_in_dim(kick_wide, 2 * block + 1, 2, 0),
            jnp.zeros((2, LANES), F32),
        ],
        axis=0,
    )
    send = call(
        lambda *r: middle_kernel(images, *r),
        shaped(images * SPAN, LANES),
        [scratch(2 * images * 8), weight_scratch(3 * images)] + [scratch(4 * images * ROWS)] * 3,
        matrix, info, got,
    )
    got = transpose(send)
    chunk = 2 * SPAN
    message = jnp.concatenate(
        [got[0:SPAN]]
        + [got[chunk + 2 * axis : chunk + 2 * axis + 1] for axis in range(3)]
        + [occupied[0:1]],
        axis=0,
    )
    message = slab_shift(message, -1)
    pos, vel = call(
        lambda *r: last_kernel(cells, *r),
        (shaped(*pos.shape), shaped(*vel.shape)),
        slab_scratch,
        got, message, edge, occupied, kick,
    )
    return pos.transpose(1, 0, 2)[None], vel.transpose(1, 0, 2)[None]


def solution(mesh):
    return jax.shard_map(
        local,
        mesh=mesh,
        in_specs=(
            P("image", "space", None, None),
            P("image", "space", None, None),
            P("space"),
            P("space", None),
            P(),
        ),
        out_specs=(P("image", "space", None, None), P("image", "space", None, None)),
        check_vma=False,
    )
```

```python
import math

import jax
import jax.numpy as jnp
import numpy as np
from jax import lax
from jax.experimental import pallas as pl
from jax.experimental.pallas import tpu as pltpu
from jax.sharding import PartitionSpec as P

STEPS = 2

time_step = 1.5
cycle_omega = 6.0
strength = 0.01
width_sq = 0.25

F32 = jnp.float32
BF16 = jnp.bfloat16
LANES = 128
ROWS = 24
SPAN = 12
GROUP = 13
WIDE = 24
ALPHA = math.sqrt(math.log2(math.e) / width_sq)
GAIN = strength / width_sq / ALPHA
FAR = 1e12


def cycle_matrix(count):
    j = np.arange(count, dtype=np.float64)[:, None]
    k = np.arange(count, dtype=np.float64)[None, :]
    half = count // 2
    phase = 2.0 * np.pi * j * k / count
    table = np.where(
        k < half, np.sqrt(2.0 / count) * np.cos(phase), np.sqrt(2.0 / count) * np.sin(phase)
    )
    table = np.where(k == 0, 1.0 / np.sqrt(count), table)
    table = np.where(k == half, np.cos(np.pi * j) / np.sqrt(count), table)
    omega = 2.0 * cycle_omega * np.sin(np.pi * k[0] / count)
    angle = omega * time_step
    to_position = np.where(k[0] == 0, time_step, np.sin(angle) / np.where(k[0] == 0, 1.0, omega))
    same = (table * np.cos(angle)) @ table.T
    from_velocity = (table * to_position) @ table.T
    from_position = (table * (-omega * np.sin(angle))) @ table.T
    return np.block([[same, from_velocity], [from_position, same]]).astype(np.float32)


def split3(value):
    high = value.astype(BF16).astype(F32)
    rest = value - high
    mid = rest.astype(BF16).astype(F32)
    low = (rest - mid).astype(BF16).astype(F32)
    return high, mid, low


def put_tables(planes, occupied, tables, start, stride=1):
    left, right, moved = tables
    count = planes[0].shape[0]
    one = jnp.ones_like(planes[0])

    def put(ref, row, value):
        ref[pl.ds(start * ROWS + row, count, stride=stride * ROWS), :] = value

    def norm(parts):
        total = parts[0] * parts[0] + parts[1] * parts[1] + parts[2] * parts[2]
        return split3(-0.5 * total - FAR * (1.0 - occupied))

    scaled = [ALPHA * plane for plane in planes]
    pieces = [split3(part) for part in scaled]
    norms = norm(scaled)
    for axis in range(3):
        high, mid, low = pieces[axis]
        for row, value in ((0, high), (4, mid), (8, high), (12, low), (16, high), (20, mid)):
            put(left, row + axis, value)
        for row, value in ((0, high), (4, high), (8, mid), (12, high), (16, low), (20, mid)):
            put(right, row + axis, value)
            if axis:
                put(moved, row + axis, value)
    for piece in range(3):
        put(left, 8 * piece + 3, norms[piece])
        put(left, 8 * piece + 7, one)
        put(right, 8 * piece + 3, one)
        put(right, 8 * piece + 7, norms[piece])
        put(moved, 8 * piece + 3, one)
    ahead = ALPHA * (planes[0] + 1.0)
    high, mid, low = split3(ahead)
    for row, value in ((0, high), (4, high), (8, mid), (12, high), (16, low), (20, mid)):
        put(moved, row, value)
    norms = norm([ahead, scaled[1], scaled[2]])
    for piece in range(3):
        put(moved, 8 * piece + 7, norms[piece])


def table_rows(ref, cell):
    return ref[cell * ROWS : (cell + 1) * ROWS, :]


def factor(table):
    pad = jnp.zeros((8, LANES), F32)
    return jnp.concatenate([table, pad], axis=0).astype(BF16)


def put_weights(tables, weights, index, own, near, full):
    left, right, moved = tables
    others = factor(table_rows(moved, near))
    if full:
        others = jnp.concatenate([factor(table_rows(right, own)), others], axis=1)
    exponent = lax.dot_general(
        factor(table_rows(left, own)),
        others,
        (((0,), (0,)), ((), ())),
        preferred_element_type=F32,
    )
    start = 0 if full else LANES
    weights[index * LANES : (index + 1) * LANES, start:] = jnp.exp2(exponent).astype(BF16)


def fold(sums):
    return sums[0:8], sums[0:8] + sums[8:16] + sums[16:24]


def own_sums(tables, weights, index, own, near):
    both = jnp.concatenate(
        [factor(table_rows(tables[1], own)), factor(table_rows(tables[2], near))], axis=1
    )
    weight = weights[index * LANES : (index + 1) * LANES, :]
    return fold(
        lax.dot_general(both, weight, (((1,), (1,)), ((), ())), preferred_element_type=F32)
    )


def next_sums(tables, weights, index, own):
    weight = weights[index * LANES : (index + 1) * LANES, LANES:]
    return fold(
        lax.dot_general(
            factor(table_rows(tables[1], own)),
            weight,
            (((1,), (0,)), ((), ())),
            preferred_element_type=F32,
        )
    )


def force_of(tables, own, sums, carry):
    table = table_rows(tables[1], own)
    place = table[0:8] + table[8:16] + table[16:24]
    total = 0.0
    if sums is not None:
        total = place * sums[0][3:4] - sums[1]
    if carry is not None:
        shift = jnp.where(lax.broadcasted_iota(jnp.int32, (8, LANES), 0) == 0, ALPHA, 0.0)
        total = total + ((place + shift) * carry[0][3:4] - carry[1])
    return GAIN * total


def chain_forces(tables, weights, steps, emit, group):
    carry = None
    for start in range(0, len(steps), group):
        part = list(enumerate(steps))[start : start + group]
        for index, (own, inner, _) in part:
            put_weights(tables, weights, index, own, own + 1, inner)
        for index, (own, inner, more) in part:
            if inner:
                sums = own_sums(tables, weights, index, own, own + 1)
                emit(own, force_of(tables, own, sums, carry))
            carry = next_sums(tables, weights, index, own) if more else None
    return carry


def scratch(rows):
    return pltpu.VMEM((rows, LANES), F32)


VMEM = pl.BlockSpec(memory_space=pltpu.VMEM)
PARAMS = pltpu.CompilerParams(vmem_limit_bytes=48 * 1024 * 1024)


def kick_of(types, mass_ref):
    mass = jnp.zeros(types.shape, F32)
    for kind in range(mass_ref.shape[0]):
        mass = mass + jnp.where(types == kind, mass_ref[kind], 0.0)
    return 0.5 * time_step / mass


def edge_kernel(cells, count_ref, mass_ref, pos_ref, vel_ref, type_ref, out_ref):
    for axis in range(3):
        out_ref[axis * 4 : axis * 4 + 4, :] = pos_ref[axis, 4:8, :]
        out_ref[12 + axis * 3 : 15 + axis * 3, :] = vel_ref[axis, 5:8, :]
    out_ref[21:24, :] = kick_of(type_ref[...], mass_ref)[5:8]
    slot = lax.broadcasted_iota(jnp.int32, (1, LANES), 1)
    for near in range(4):
        occupied = (slot < count_ref[cells - 4 + near]).astype(F32)
        out_ref[24 + near : 25 + near, :] = occupied
    out_ref[28:32, :] = jnp.zeros((4, LANES), F32)


def add_kick(place, speed):
    def emit(slot, force):
        rows = slice(slot * 8, slot * 8 + 8)
        speed[rows, :] = speed[rows, :] + place[rows, :][3:4] * force

    return emit


def first_inner_kernel(
    cells, pos_ref, vel_ref, occ_ref, kick_ref, place, speed, weights, left, right, moved
):
    for axis in range(3):
        place[pl.ds(4 * 8 + axis, cells, stride=8), :] = pos_ref[axis]
        speed[pl.ds(4 * 8 + axis, cells, stride=8), :] = vel_ref[axis]
    place[pl.ds(4 * 8 + 3, cells, stride=8), :] = kick_ref[...]
    tables = (left, right, moved)
    put_tables([pos_ref[axis] for axis in range(3)], occ_ref[...], tables, 4)
    steps = [(own, True, own < cells + 2) for own in range(4, cells + 3)]
    chain_forces(tables, weights, steps, add_kick(place, speed), GROUP)


def first_outer_kernel(
    cells, edge_ref, occ_ref, place_ref, speed_ref, send_ref,
    place, speed, weights, left, right, moved,
):
    half = cells // 4
    place[32:, :] = place_ref[32:, :]
    speed[32:, :] = speed_ref[32:, :]
    for axis in range(3):
        place[pl.ds(axis, 4, stride=8), :] = edge_ref[axis * 4 : axis * 4 + 4, :]
        speed[pl.ds(8 + axis, 3, stride=8), :] = edge_ref[12 + axis * 3 : 15 + axis * 3, :]
    place[pl.ds(8 + 3, 3, stride=8), :] = edge_ref[21:24, :]
    tables = (left, right, moved)
    planes = [place[pl.ds(axis, 8, stride=8), :] for axis in range(3)]
    occupied = jnp.concatenate([edge_ref[24:28, :], occ_ref[0:4, :]], axis=0)
    put_tables(planes, occupied, tables, 0)
    emit = add_kick(place, speed)
    carry = chain_forces(
        tables, weights, [(own, own > 0, True) for own in range(4)], emit, GROUP
    )
    emit(4, force_of(tables, 4, None, carry))
    for kind, source in enumerate((place, speed)):
        for axis in range(3):
            for near in range(4):
                row = (kind * 3 + axis) * 4 + near
                for part in range(2):
                    first = (part * 2 * half + 1 + near) * 8 + axis
                    send_ref[pl.ds(part * WIDE + row, half, stride=2 * WIDE), :] = source[
                        pl.ds(first, half, stride=16), :
                    ]


def cycle(matrix, blocks):
    return jnp.dot(
        matrix,
        jnp.concatenate(blocks, axis=1),
        precision=lax.Precision.HIGHEST,
        preferred_element_type=F32,
    )


def lanes_of(array, index):
    return array[:, index * LANES : (index + 1) * LANES]


def middle_kernel(
    images, matrix_ref, info_ref, got_ref, send_ref, forces, weights, left, right, moved
):
    tables = (left, right, moved)

    def blocks_of(slots):
        return [
            jnp.concatenate(
                [
                    got_ref[pl.ds((kind * 3 + axis) * 4 + slot, images, stride=WIDE), :]
                    for kind in range(2)
                ],
                axis=0,
            )
            for slot in slots
            for axis in range(3)
        ]

    inner = cycle(matrix_ref[...], blocks_of((1, 2)))
    outer = cycle(matrix_ref[:images, :], blocks_of((0, 3)))
    for slot in range(4):
        source, first = ((outer, 0), (inner, 0), (inner, 3), (outer, 3))[slot]
        planes = [lanes_of(source, first + axis)[:images] for axis in range(3)]
        occupied = jnp.broadcast_to(info_ref[slot : slot + 1, :], (images, LANES))
        put_tables(planes, occupied, tables, slot, stride=4)

    def emit(cell, force):
        row = (cell // 4 * 2 + cell % 4 - 1) * 8
        forces[row : row + 8, :] = force

    steps = [
        (4 * image + slot, slot > 0, slot < 2) for image in range(images) for slot in range(3)
    ]
    chain_forces(tables, weights, steps, emit, GROUP)
    blocks = []
    for parity in range(2):
        kick = 2.0 * info_ref[4 + parity : 5 + parity, :]
        for axis in range(3):
            now = lanes_of(inner, parity * 3 + axis)
            force = forces[pl.ds(parity * 8 + axis, images, stride=16), :]
            blocks.append(jnp.concatenate([now[:images], now[images:] + kick * force], axis=0))
    ahead = cycle(matrix_ref[...], blocks)
    for parity in range(2):
        for axis in range(3):
            after = lanes_of(ahead, parity * 3 + axis)
            for kind in range(2):
                row = (kind * 3 + axis) * 2 + parity
                send_ref[pl.ds(row, images, stride=SPAN), :] = after[
                    kind * images : (kind + 1) * images
                ]


def last_inner_kernel(
    cells, got_ref, first_ref, occ_ref, kick_ref, place, speed,
    occ_all, weights, left, right, moved,
):
    half = cells // 4
    for kind, target in enumerate((place, speed)):
        for axis in range(3):
            for parity in range(2):
                row = (kind * 3 + axis) * 2 + parity
                for part in range(2):
                    first = (part * 2 * half + parity) * 8 + axis
                    target[pl.ds(first, half, stride=16), :] = got_ref[
                        pl.ds(part * SPAN + row, half, stride=2 * SPAN), :
                    ]
    place[pl.ds(2 * 8 + 3, cells, stride=8), :] = kick_ref[...]
    occ_all[0:2, :] = first_ref[26:28, :]
    occ_all[2:cells, :] = occ_ref[: cells - 2, :]
    tables = (left, right, moved)
    planes = [place[pl.ds(axis, cells, stride=8), :] for axis in range(3)]
    put_tables(planes, occ_all[...], tables, 0)
    emit = add_kick(place, speed)
    steps = [(own, own > 1, True) for own in range(1, cells - 1)]
    carry = chain_forces(tables, weights, steps, emit, GROUP)
    emit(cells - 1, force_of(tables, cells - 1, None, carry))


def last_outer_kernel(
    cells, edge_ref, occ_ref, place_ref, speed_ref, pos_ref, vel_ref,
    place, speed, weights, left, right, moved,
):
    base = cells - 8
    place[0:64, :] = place_ref[base * 8 : cells * 8, :]
    speed[0:64, :] = speed_ref[base * 8 : cells * 8, :]
    for axis in range(3):
        for parity in range(2):
            slot = (8 + parity) * 8 + axis
            row = axis * 2 + parity
            place[slot : slot + 1, :] = edge_ref[row : row + 1, :]
            speed[slot : slot + 1, :] = edge_ref[row + 6 : row + 7, :]
        slot = 10 * 8 + axis
        place[slot : slot + 1, :] = edge_ref[12 + axis : 13 + axis, :]
    for parity in range(2):
        slot = (8 + parity) * 8 + 3
        place[slot : slot + 1, :] = place_ref[
            (cells + parity) * 8 + 3 : (cells + parity) * 8 + 4, :
        ]
    tables = (left, right, moved)
    planes = [place[pl.ds(axis, 16, stride=8), :] for axis in range(3)]
    occupied = jnp.concatenate(
        [
            jnp.zeros((7, LANES), F32),
            occ_ref[cells - 3 : cells, :],
            edge_ref[15:16, :],
            jnp.zeros((5, LANES), F32),
        ],
        axis=0,
    )
    put_tables(planes, occupied, tables, 0)
    steps = [(own, True, own < 9) for own in range(7, 10)]
    chain_forces(tables, weights, steps, add_kick(place, speed), GROUP)
    for axis in range(3):
        for out_ref, whole, end in ((pos_ref, place_ref, place), (vel_ref, speed_ref, speed)):
            out_ref[axis, 0 : base, :] = whole[pl.ds(2 * 8 + axis, base, stride=8), :]
            out_ref[axis, base:cells, :] = end[pl.ds(2 * 8 + axis, 8, stride=8), :]


def local(positions, velocities, counts, types, masses):
    images = lax.axis_size("image")
    slabs = lax.axis_size("space")
    cells = positions.shape[1]
    rows = cells + 8

    def slab_shift(array, distance):
        pairs = [(s, (s + distance) % slabs) for s in range(slabs)]
        return lax.ppermute(array, "space", pairs)

    def transpose(array):
        blocks = array.reshape(images, array.shape[0] // images // 4, 4, LANES)
        blocks = lax.all_to_all(blocks, "image", split_axis=0, concat_axis=0, tiled=True)
        return blocks.reshape(array.shape)

    def call(kernel, outs, scratches, *args):
        return pl.pallas_call(
            kernel,
            out_shape=outs,
            in_specs=[VMEM] * len(args),
            out_specs=jax.tree.map(lambda _: VMEM, outs),
            scratch_shapes=scratches,
            compiler_params=PARAMS,
            cost_estimate=pl.CostEstimate(
                flops=20_000_000_000, bytes_accessed=1_000_000, transcendentals=0
            ),
        )(*args)

    def shaped(*shape):
        return jax.ShapeDtypeStruct(shape, F32)

    def weight_scratch(steps):
        return pltpu.VMEM((steps * LANES, 2 * LANES), BF16)

    slot_index = lax.broadcasted_iota(jnp.int32, types.shape, 1)
    occupied = (slot_index < counts[:, None]).astype(F32)
    type_index = lax.broadcasted_iota(jnp.int32, (masses.shape[0],) + types.shape, 0)
    chosen = jnp.sum(jnp.where(types[None] == type_index, masses[:, None, None], 0.0), axis=0)
    kick = 0.5 * time_step * (1.0 / chosen)
    matrix = jnp.asarray(cycle_matrix(images))
    group = lax.axis_index("image")
    block = (group % 2) * (images // 2) + group // 2

    pos = positions[0].transpose(1, 0, 2)
    vel = velocities[0].transpose(1, 0, 2)
    window = shaped(rows * 8, LANES)
    slab_scratch = [weight_scratch(cells)] + [scratch(rows * ROWS)] * 3
    edge_scratch = [scratch(rows * 8)] * 2 + [weight_scratch(8)] + [scratch(16 * ROWS)] * 3
    last = cells // 8 - 1
    smem = pl.BlockSpec(memory_space=pltpu.SMEM)
    edge = pl.pallas_call(
        lambda *r: edge_kernel(cells, *r),
        grid=(1,),
        out_shape=shaped(32, LANES),
        in_specs=[
            smem,
            smem,
            pl.BlockSpec((3, 8, LANES), lambda i: (0, last, 0)),
            pl.BlockSpec((3, 8, LANES), lambda i: (0, last, 0)),
            pl.BlockSpec((8, LANES), lambda i: (last, 0)),
        ],
        out_specs=pl.BlockSpec((32, LANES), lambda i: (0, 0)),
        compiler_params=PARAMS,
    )(counts, masses, pos, vel, types)
    edge = slab_shift(edge, 1)
    place, speed = call(
        lambda *r: first_inner_kernel(cells, *r),
        (window, window),
        slab_scratch,
        pos, vel, occupied, kick,
    )
    send = call(
        lambda *r: first_outer_kernel(cells, *r),
        shaped(images * WIDE, LANES),
        edge_scratch,
        edge, occupied, place, speed,
    )
    got = transpose(send)
    occ_wide = jnp.concatenate([edge[24:28], occupied], axis=0)
    kick_wide = jnp.concatenate([edge[21:24], kick], axis=0)
    info = jnp.concatenate(
        [
            lax.dynamic_slice_in_dim(occ_wide, 2 * block + 1, 4, 0),
            lax.dynamic_slice_in_dim(kick_wide, 2 * block + 1, 2, 0),
            jnp.zeros((2, LANES), F32),
        ],
        axis=0,
    )
    send = call(
        lambda *r: middle_kernel(images, *r),
        shaped(images * SPAN, LANES),
        [scratch(2 * images * 8), weight_scratch(3 * images)] + [scratch(4 * images * ROWS)] * 3,
        matrix, info, got,
    )
    got = transpose(send)
    chunk = 2 * SPAN
    message = jnp.concatenate(
        [got[0:SPAN]]
        + [got[chunk + 2 * axis : chunk + 2 * axis + 1] for axis in range(3)]
        + [occupied[0:1]],
        axis=0,
    )
    message = slab_shift(message, -1)
    place, speed = call(
        lambda *r: last_inner_kernel(cells, *r),
        (window, window),
        [scratch(cells)] + slab_scratch,
        got, edge, occupied, kick,
    )
    pos, vel = call(
        lambda *r: last_outer_kernel(cells, *r),
        (shaped(*pos.shape), shaped(*vel.shape)),
        edge_scratch,
        message, occupied, place, speed,
    )
    return pos.transpose(1, 0, 2)[None], vel.transpose(1, 0, 2)[None]


def solution(mesh):
    return jax.shard_map(
        local,
        mesh=mesh,
        in_specs=(
            P("image", "space", None, None),
            P("image", "space", None, None),
            P("space"),
            P("space", None),
            P(),
        ),
        out_specs=(P("image", "space", None, None), P("image", "space", None, None)),
        check_vma=False,
    )
```

```python
import math

import jax
import jax.numpy as jnp
import numpy as np
from jax import lax
from jax.experimental import pallas as pl
from jax.experimental.pallas import tpu as pltpu
from jax.sharding import PartitionSpec as P

STEPS = 2

time_step = 1.5
cycle_omega = 6.0
strength = 0.01
width_sq = 0.25

F32 = jnp.float32
BF16 = jnp.bfloat16
LANES = 128
ROWS = 24
SPAN = 12
GROUP = 13
WIDE = 24
ALPHA = math.sqrt(math.log2(math.e) / width_sq)
GAIN = strength / width_sq / ALPHA
FAR = 1e12


def cycle_matrix(count):
    j = np.arange(count, dtype=np.float64)[:, None]
    k = np.arange(count, dtype=np.float64)[None, :]
    half = count // 2
    phase = 2.0 * np.pi * j * k / count
    table = np.where(
        k < half, np.sqrt(2.0 / count) * np.cos(phase), np.sqrt(2.0 / count) * np.sin(phase)
    )
    table = np.where(k == 0, 1.0 / np.sqrt(count), table)
    table = np.where(k == half, np.cos(np.pi * j) / np.sqrt(count), table)
    omega = 2.0 * cycle_omega * np.sin(np.pi * k[0] / count)
    angle = omega * time_step
    to_position = np.where(k[0] == 0, time_step, np.sin(angle) / np.where(k[0] == 0, 1.0, omega))
    same = (table * np.cos(angle)) @ table.T
    from_velocity = (table * to_position) @ table.T
    from_position = (table * (-omega * np.sin(angle))) @ table.T
    return np.block([[same, from_velocity], [from_position, same]]).astype(np.float32)


def split3(value):
    high = value.astype(BF16).astype(F32)
    rest = value - high
    mid = rest.astype(BF16).astype(F32)
    low = (rest - mid).astype(BF16).astype(F32)
    return high, mid, low


def put_tables(planes, occupied, tables, start, sides="lrm"):
    left, right, moved = tables
    count = planes[0].shape[0]
    one = jnp.ones_like(planes[0])

    def put(ref, row, value):
        ref[pl.ds(start * ROWS + row, count, stride=ROWS), :] = value

    def norm(parts):
        total = parts[0] * parts[0] + parts[1] * parts[1] + parts[2] * parts[2]
        return split3(-0.5 * total - FAR * (1.0 - occupied))

    def put_right(ref, pieces, norms):
        for axis in range(3):
            high, mid, low = pieces[axis]
            for row, value in ((0, high), (4, high), (8, mid), (12, high), (16, low), (20, mid)):
                put(ref, row + axis, value)
        for piece in range(3):
            put(ref, 8 * piece + 3, one)
            put(ref, 8 * piece + 7, norms[piece])

    scaled = [ALPHA * plane for plane in planes]
    pieces = [split3(part) for part in scaled]
    if "l" in sides:
        norms = norm(scaled)
        for axis in range(3):
            high, mid, low = pieces[axis]
            for row, value in ((0, high), (4, mid), (8, high), (12, low), (16, high), (20, mid)):
                put(left, row + axis, value)
        for piece in range(3):
            put(left, 8 * piece + 3, norms[piece])
            put(left, 8 * piece + 7, one)
        put_right(right, pieces, norms)
    if "m" in sides:
        ahead = ALPHA * (planes[0] + 1.0)
        put_right(moved, [split3(ahead)] + pieces[1:], norm([ahead, scaled[1], scaled[2]]))


def table_rows(ref, cell):
    return ref[cell * ROWS : (cell + 1) * ROWS, :]


def factor(table):
    pad = jnp.zeros((8, LANES), F32)
    return jnp.concatenate([table, pad], axis=0).astype(BF16)


def put_weights(tables, weights, index, own, near, full):
    left, right, moved = tables
    others = factor(table_rows(moved, near))
    if full:
        others = jnp.concatenate([factor(table_rows(right, own)), others], axis=1)
    exponent = lax.dot_general(
        factor(table_rows(left, own)),
        others,
        (((0,), (0,)), ((), ())),
        preferred_element_type=F32,
    )
    start = 0 if full else LANES
    weights[index * LANES : (index + 1) * LANES, start:] = jnp.exp2(exponent).astype(BF16)


def fold(sums):
    return sums[0:8], sums[0:8] + sums[8:16] + sums[16:24]


def own_sums(tables, weights, index, own, near):
    both = jnp.concatenate(
        [factor(table_rows(tables[1], own)), factor(table_rows(tables[2], near))], axis=1
    )
    weight = weights[index * LANES : (index + 1) * LANES, :]
    return fold(
        lax.dot_general(both, weight, (((1,), (1,)), ((), ())), preferred_element_type=F32)
    )


def next_sums(tables, weights, index, own):
    weight = weights[index * LANES : (index + 1) * LANES, LANES:]
    return fold(
        lax.dot_general(
            factor(table_rows(tables[1], own)),
            weight,
            (((1,), (0,)), ((), ())),
            preferred_element_type=F32,
        )
    )


def force_of(tables, own, sums, carry):
    table = table_rows(tables[1], own)
    place = table[0:8] + table[8:16] + table[16:24]
    total = 0.0
    if sums is not None:
        total = place * sums[0][3:4] - sums[1]
    if carry is not None:
        shift = jnp.where(lax.broadcasted_iota(jnp.int32, (8, LANES), 0) == 0, ALPHA, 0.0)
        total = total + ((place + shift) * carry[0][3:4] - carry[1])
    return GAIN * total


def chain_forces(tables, weights, steps, emit, group, ahead=1):
    carry = None
    for start in range(0, len(steps), group):
        part = list(enumerate(steps))[start : start + group]
        for index, (own, inner, _) in part:
            put_weights(tables, weights, index, own, own + ahead, inner)
        for index, (own, inner, more) in part:
            if inner:
                sums = own_sums(tables, weights, index, own, own + ahead)
                emit(own, force_of(tables, own, sums, carry))
            carry = next_sums(tables, weights, index, own) if more else None
    return carry


def scratch(rows):
    return pltpu.VMEM((rows, LANES), F32)


VMEM = pl.BlockSpec(memory_space=pltpu.VMEM)
PARAMS = pltpu.CompilerParams(vmem_limit_bytes=48 * 1024 * 1024)


def kick_of(types, mass_ref):
    mass = jnp.zeros(types.shape, F32)
    for kind in range(mass_ref.shape[0]):
        mass = mass + jnp.where(types == kind, mass_ref[kind], 0.0)
    return 0.5 * time_step / mass


def edge_kernel(cells, count_ref, mass_ref, pos_ref, vel_ref, type_ref, out_ref):
    for axis in range(3):
        out_ref[axis * 4 : axis * 4 + 4, :] = pos_ref[axis, 4:8, :]
        out_ref[12 + axis * 3 : 15 + axis * 3, :] = vel_ref[axis, 5:8, :]
    out_ref[21:24, :] = kick_of(type_ref[...], mass_ref)[5:8]
    slot = lax.broadcasted_iota(jnp.int32, (1, LANES), 1)
    for near in range(4):
        occupied = (slot < count_ref[cells - 4 + near]).astype(F32)
        out_ref[24 + near : 25 + near, :] = occupied
    out_ref[28:32, :] = jnp.zeros((4, LANES), F32)


def add_kick(place, speed):
    def emit(slot, force):
        rows = slice(slot * 8, slot * 8 + 8)
        speed[rows, :] = speed[rows, :] + place[rows, :][3:4] * force

    return emit


def first_inner_kernel(
    cells, pos_ref, vel_ref, occ_ref, kick_ref, place, speed, weights, left, right, moved
):
    for axis in range(3):
        place[pl.ds(4 * 8 + axis, cells, stride=8), :] = pos_ref[axis]
        speed[pl.ds(4 * 8 + axis, cells, stride=8), :] = vel_ref[axis]
    place[pl.ds(4 * 8 + 3, cells, stride=8), :] = kick_ref[...]
    tables = (left, right, moved)
    put_tables([pos_ref[axis] for axis in range(3)], occ_ref[...], tables, 4)
    steps = [(own, True, own < cells + 2) for own in range(4, cells + 3)]
    chain_forces(tables, weights, steps, add_kick(place, speed), GROUP)


def first_outer_kernel(
    cells, edge_ref, occ_ref, place_ref, speed_ref, send_ref,
    place, speed, weights, left, right, moved,
):
    half = cells // 4
    place[32:, :] = place_ref[32:, :]
    speed[32:, :] = speed_ref[32:, :]
    for axis in range(3):
        place[pl.ds(axis, 4, stride=8), :] = edge_ref[axis * 4 : axis * 4 + 4, :]
        speed[pl.ds(8 + axis, 3, stride=8), :] = edge_ref[12 + axis * 3 : 15 + axis * 3, :]
    place[pl.ds(8 + 3, 3, stride=8), :] = edge_ref[21:24, :]
    tables = (left, right, moved)
    planes = [place[pl.ds(axis, 8, stride=8), :] for axis in range(3)]
    occupied = jnp.concatenate([edge_ref[24:28, :], occ_ref[0:4, :]], axis=0)
    put_tables(planes, occupied, tables, 0)
    emit = add_kick(place, speed)
    carry = chain_forces(
        tables, weights, [(own, own > 0, True) for own in range(4)], emit, GROUP
    )
    emit(4, force_of(tables, 4, None, carry))
    for kind, source in enumerate((place, speed)):
        for axis in range(3):
            for near in range(4):
                row = (kind * 3 + axis) * 4 + near
                for part in range(2):
                    first = (part * 2 * half + 1 + near) * 8 + axis
                    send_ref[pl.ds(part * WIDE + row, half, stride=2 * WIDE), :] = source[
                        pl.ds(first, half, stride=16), :
                    ]


def cycle(matrix, blocks):
    return jnp.dot(
        matrix,
        jnp.concatenate(blocks, axis=1),
        precision=lax.Precision.HIGHEST,
        preferred_element_type=F32,
    )


def lanes_of(array, index):
    return array[:, index * LANES : (index + 1) * LANES]


def middle_kernel(
    images, matrix_ref, info_ref, got_ref, send_ref, forces, weights, left, right, moved
):
    tables = (left, right, moved)

    def blocks_of(slots):
        return [
            jnp.concatenate(
                [
                    got_ref[pl.ds((kind * 3 + axis) * 4 + slot, images, stride=WIDE), :]
                    for kind in range(2)
                ],
                axis=0,
            )
            for slot in slots
            for axis in range(3)
        ]

    inner = cycle(matrix_ref[...], blocks_of((1, 2)))
    outer = cycle(matrix_ref[:images, :], blocks_of((0, 3)))
    for slot in range(4):
        source, first = ((outer, 0), (inner, 0), (inner, 3), (outer, 3))[slot]
        planes = [lanes_of(source, first + axis)[:images] for axis in range(3)]
        occupied = jnp.broadcast_to(info_ref[slot : slot + 1, :], (images, LANES))
        put_tables(planes, occupied, tables, slot * images, ("lr", "lrm", "lrm", "m")[slot])

    def emit(cell, force):
        row = (cell - images) * 8
        forces[row : row + 8, :] = force

    steps = [
        (slot * images + image, slot > 0, slot < 2)
        for image in range(images)
        for slot in range(3)
    ]
    chain_forces(tables, weights, steps, emit, 12, ahead=images)
    blocks = []
    for parity in range(2):
        kick = 2.0 * info_ref[4 + parity : 5 + parity, :]
        for axis in range(3):
            now = lanes_of(inner, parity * 3 + axis)
            force = forces[pl.ds(parity * images * 8 + axis, images, stride=8), :]
            blocks.append(jnp.concatenate([now[:images], now[images:] + kick * force], axis=0))
    ahead = cycle(matrix_ref[...], blocks)
    for parity in range(2):
        for axis in range(3):
            after = lanes_of(ahead, parity * 3 + axis)
            for kind in range(2):
                row = (kind * 3 + axis) * 2 + parity
                send_ref[pl.ds(row, images, stride=SPAN), :] = after[
                    kind * images : (kind + 1) * images
                ]


def last_inner_kernel(
    cells, got_ref, first_ref, occ_ref, kick_ref, place, speed,
    occ_all, weights, left, right, moved,
):
    half = cells // 4
    for kind, target in enumerate((place, speed)):
        for axis in range(3):
            for parity in range(2):
                row = (kind * 3 + axis) * 2 + parity
                for part in range(2):
                    first = (part * 2 * half + parity) * 8 + axis
                    target[pl.ds(first, half, stride=16), :] = got_ref[
                        pl.ds(part * SPAN + row, half, stride=2 * SPAN), :
                    ]
    place[pl.ds(2 * 8 + 3, cells, stride=8), :] = kick_ref[...]
    occ_all[0:2, :] = first_ref[26:28, :]
    occ_all[2:cells, :] = occ_ref[: cells - 2, :]
    tables = (left, right, moved)
    planes = [place[pl.ds(axis, cells, stride=8), :] for axis in range(3)]
    put_tables(planes, occ_all[...], tables, 0)
    emit = add_kick(place, speed)
    steps = [(own, own > 1, True) for own in range(1, cells - 1)]
    carry = chain_forces(tables, weights, steps, emit, GROUP)
    emit(cells - 1, force_of(tables, cells - 1, None, carry))


def last_outer_kernel(
    cells, edge_ref, occ_ref, place_ref, speed_ref, pos_ref, vel_ref,
    place, speed, weights, left, right, moved,
):
    base = cells - 8
    place[0:64, :] = place_ref[base * 8 : cells * 8, :]
    speed[0:64, :] = speed_ref[base * 8 : cells * 8, :]
    for axis in range(3):
        for parity in range(2):
            slot = (8 + parity) * 8 + axis
            row = axis * 2 + parity
            place[slot : slot + 1, :] = edge_ref[row : row + 1, :]
            speed[slot : slot + 1, :] = edge_ref[row + 6 : row + 7, :]
        slot = 10 * 8 + axis
        place[slot : slot + 1, :] = edge_ref[12 + axis : 13 + axis, :]
    for parity in range(2):
        slot = (8 + parity) * 8 + 3
        place[slot : slot + 1, :] = place_ref[
            (cells + parity) * 8 + 3 : (cells + parity) * 8 + 4, :
        ]
    tables = (left, right, moved)
    planes = [place[pl.ds(axis, 16, stride=8), :] for axis in range(3)]
    occupied = jnp.concatenate(
        [
            jnp.zeros((7, LANES), F32),
            occ_ref[cells - 3 : cells, :],
            edge_ref[15:16, :],
            jnp.zeros((5, LANES), F32),
        ],
        axis=0,
    )
    put_tables(planes, occupied, tables, 0)
    steps = [(own, True, own < 9) for own in range(7, 10)]
    chain_forces(tables, weights, steps, add_kick(place, speed), GROUP)
    for axis in range(3):
        for out_ref, whole, end in ((pos_ref, place_ref, place), (vel_ref, speed_ref, speed)):
            out_ref[axis, 0 : base, :] = whole[pl.ds(2 * 8 + axis, base, stride=8), :]
            out_ref[axis, base:cells, :] = end[pl.ds(2 * 8 + axis, 8, stride=8), :]


def local(positions, velocities, counts, types, masses):
    images = lax.axis_size("image")
    slabs = lax.axis_size("space")
    cells = positions.shape[1]
    rows = cells + 8

    def slab_shift(array, distance):
        pairs = [(s, (s + distance) % slabs) for s in range(slabs)]
        return lax.ppermute(array, "space", pairs)

    def transpose(array):
        blocks = array.reshape(images, array.shape[0] // images // 4, 4, LANES)
        blocks = lax.all_to_all(blocks, "image", split_axis=0, concat_axis=0, tiled=True)
        return blocks.reshape(array.shape)

    def call(kernel, outs, scratches, *args):
        return pl.pallas_call(
            kernel,
            out_shape=outs,
            in_specs=[VMEM] * len(args),
            out_specs=jax.tree.map(lambda _: VMEM, outs),
            scratch_shapes=scratches,
            compiler_params=PARAMS,
            cost_estimate=pl.CostEstimate(
                flops=20_000_000_000, bytes_accessed=1_000_000, transcendentals=0
            ),
        )(*args)

    def shaped(*shape):
        return jax.ShapeDtypeStruct(shape, F32)

    def weight_scratch(steps):
        return pltpu.VMEM((steps * LANES, 2 * LANES), BF16)

    slot_index = lax.broadcasted_iota(jnp.int32, types.shape, 1)
    occupied = (slot_index < counts[:, None]).astype(F32)
    type_index = lax.broadcasted_iota(jnp.int32, (masses.shape[0],) + types.shape, 0)
    chosen = jnp.sum(jnp.where(types[None] == type_index, masses[:, None, None], 0.0), axis=0)
    kick = 0.5 * time_step * (1.0 / chosen)
    matrix = jnp.asarray(cycle_matrix(images))
    group = lax.axis_index("image")
    block = (group % 2) * (images // 2) + group // 2

    pos = positions[0].transpose(1, 0, 2)
    vel = velocities[0].transpose(1, 0, 2)
    window = shaped(rows * 8, LANES)
    slab_scratch = [weight_scratch(cells)] + [scratch(rows * ROWS)] * 3
    edge_scratch = [scratch(rows * 8)] * 2 + [weight_scratch(8)] + [scratch(16 * ROWS)] * 3
    last = cells // 8 - 1
    smem = pl.BlockSpec(memory_space=pltpu.SMEM)
    edge = pl.pallas_call(
        lambda *r: edge_kernel(cells, *r),
        grid=(1,),
        out_shape=shaped(32, LANES),
        in_specs=[
            smem,
            smem,
            pl.BlockSpec((3, 8, LANES), lambda i: (0, last, 0)),
            pl.BlockSpec((3, 8, LANES), lambda i: (0, last, 0)),
            pl.BlockSpec((8, LANES), lambda i: (last, 0)),
        ],
        out_specs=pl.BlockSpec((32, LANES), lambda i: (0, 0)),
        compiler_params=pltpu.CompilerParams(vmem_limit_bytes=62 * 1024 * 1024),
    )(counts, masses, pos, vel, types)
    edge = slab_shift(edge, 1)
    place, speed = call(
        lambda *r: first_inner_kernel(cells, *r),
        (window, window),
        slab_scratch,
        pos, vel, occupied, kick,
    )
    send = call(
        lambda *r: first_outer_kernel(cells, *r),
        shaped(images * WIDE, LANES),
        edge_scratch,
        edge, occupied, place, speed,
    )
    got = transpose(send)
    occ_wide = jnp.concatenate([edge[24:28], occupied], axis=0)
    kick_wide = jnp.concatenate([edge[21:24], kick], axis=0)
    info = jnp.concatenate(
        [
            lax.dynamic_slice_in_dim(occ_wide, 2 * block + 1, 4, 0),
            lax.dynamic_slice_in_dim(kick_wide, 2 * block + 1, 2, 0),
            jnp.zeros((2, LANES), F32),
        ],
        axis=0,
    )
    send = call(
        lambda *r: middle_kernel(images, *r),
        shaped(images * SPAN, LANES),
        [scratch(2 * images * 8), weight_scratch(3 * images)] + [scratch(4 * images * ROWS)] * 3,
        matrix, info, got,
    )
    got = transpose(send)
    chunk = 2 * SPAN
    message = jnp.concatenate(
        [got[0:SPAN]]
        + [got[chunk + 2 * axis : chunk + 2 * axis + 1] for axis in range(3)]
        + [occupied[0:1]],
        axis=0,
    )
    message = slab_shift(message, -1)
    place, speed = call(
        lambda *r: last_inner_kernel(cells, *r),
        (window, window),
        [scratch(cells)] + slab_scratch,
        got, edge, occupied, kick,
    )
    pos, vel = call(
        lambda *r: last_outer_kernel(cells, *r),
        (shaped(*pos.shape), shaped(*vel.shape)),
        edge_scratch,
        message, occupied, place, speed,
    )
    return pos.transpose(1, 0, 2)[None], vel.transpose(1, 0, 2)[None]


def solution(mesh):
    return jax.shard_map(
        local,
        mesh=mesh,
        in_specs=(
            P("image", "space", None, None),
            P("image", "space", None, None),
            P("space"),
            P("space", None),
            P(),
        ),
        out_specs=(P("image", "space", None, None), P("image", "space", None, None)),
        check_vma=False,
    )
```

```python
import math

import jax
import jax.numpy as jnp
import ml_dtypes
import numpy as np
from jax import lax
from jax.experimental import pallas as pl
from jax.experimental.pallas import tpu as pltpu
from jax.sharding import PartitionSpec as P

STEPS = 2

time_step = 1.5
cycle_omega = 6.0
strength = 0.01
width_sq = 0.25

F32 = jnp.float32
BF16 = jnp.bfloat16
LANES = 128
ROWS = 24
SPAN = 12
GROUP = 13
WIDE = 24
ALPHA = math.sqrt(math.log2(math.e) / width_sq)
GAIN = strength / width_sq / ALPHA
FAR = 1e12


def cycle_matrix(count):
    j = np.arange(count, dtype=np.float64)[:, None]
    k = np.arange(count, dtype=np.float64)[None, :]
    half = count // 2
    phase = 2.0 * np.pi * j * k / count
    table = np.where(
        k < half, np.sqrt(2.0 / count) * np.cos(phase), np.sqrt(2.0 / count) * np.sin(phase)
    )
    table = np.where(k == 0, 1.0 / np.sqrt(count), table)
    table = np.where(k == half, np.cos(np.pi * j) / np.sqrt(count), table)
    omega = 2.0 * cycle_omega * np.sin(np.pi * k[0] / count)
    angle = omega * time_step
    to_position = np.where(k[0] == 0, time_step, np.sin(angle) / np.where(k[0] == 0, 1.0, omega))
    same = (table * np.cos(angle)) @ table.T
    from_velocity = (table * to_position) @ table.T
    from_position = (table * (-omega * np.sin(angle))) @ table.T
    matrix = np.block([[same, from_velocity], [from_position, same]])
    high = matrix.astype(ml_dtypes.bfloat16)
    low = (matrix - high.astype(np.float64)).astype(ml_dtypes.bfloat16)
    return np.concatenate([high, high, low], axis=1)


def split3(value):
    high = value.astype(BF16).astype(F32)
    rest = value - high
    mid = rest.astype(BF16).astype(F32)
    low = (rest - mid).astype(BF16).astype(F32)
    return high, mid, low


def put_tables(planes, occupied, tables, start, sides="lrm"):
    left, right, moved = tables
    count = planes[0].shape[0]
    one = jnp.ones_like(planes[0])

    def put(ref, row, value):
        ref[pl.ds(start * ROWS + row, count, stride=ROWS), :] = value

    def norm(parts):
        total = parts[0] * parts[0] + parts[1] * parts[1] + parts[2] * parts[2]
        return split3(-0.5 * total - FAR * (1.0 - occupied))

    def put_right(ref, pieces, norms):
        for axis in range(3):
            high, mid, low = pieces[axis]
            for row, value in ((0, high), (4, high), (8, mid), (12, high), (16, low), (20, mid)):
                put(ref, row + axis, value)
        for piece in range(3):
            put(ref, 8 * piece + 3, one)
            put(ref, 8 * piece + 7, norms[piece])

    scaled = [ALPHA * plane for plane in planes]
    pieces = [split3(part) for part in scaled]
    if "l" in sides:
        norms = norm(scaled)
        for axis in range(3):
            high, mid, low = pieces[axis]
            for row, value in ((0, high), (4, mid), (8, high), (12, low), (16, high), (20, mid)):
                put(left, row + axis, value)
        for piece in range(3):
            put(left, 8 * piece + 3, norms[piece])
            put(left, 8 * piece + 7, one)
        put_right(right, pieces, norms)
    if "m" in sides:
        ahead = ALPHA * (planes[0] + 1.0)
        put_right(moved, [split3(ahead)] + pieces[1:], norm([ahead, scaled[1], scaled[2]]))


def table_rows(ref, cell):
    return ref[cell * ROWS : (cell + 1) * ROWS, :]


def factor(table):
    pad = jnp.zeros((8, LANES), F32)
    return jnp.concatenate([table, pad], axis=0).astype(BF16)


def put_weights(tables, weights, index, own, near, full):
    left, right, moved = tables
    others = factor(table_rows(moved, near))
    if full:
        others = jnp.concatenate([factor(table_rows(right, own)), others], axis=1)
    exponent = lax.dot_general(
        factor(table_rows(left, own)),
        others,
        (((0,), (0,)), ((), ())),
        preferred_element_type=F32,
    )
    start = 0 if full else LANES
    weights[index * LANES : (index + 1) * LANES, start:] = jnp.exp2(exponent).astype(BF16)


def fold(sums):
    return sums[0:8], sums[0:8] + sums[8:16] + sums[16:24]


def own_sums(tables, weights, index, own, near):
    both = jnp.concatenate(
        [factor(table_rows(tables[1], own)), factor(table_rows(tables[2], near))], axis=1
    )
    weight = weights[index * LANES : (index + 1) * LANES, :]
    return fold(
        lax.dot_general(both, weight, (((1,), (1,)), ((), ())), preferred_element_type=F32)
    )


def next_sums(tables, weights, index, own):
    weight = weights[index * LANES : (index + 1) * LANES, LANES:]
    return fold(
        lax.dot_general(
            factor(table_rows(tables[1], own)),
            weight,
            (((1,), (0,)), ((), ())),
            preferred_element_type=F32,
        )
    )


def force_of(tables, own, sums, carry):
    table = table_rows(tables[1], own)
    place = table[0:8] + table[8:16] + table[16:24]
    total = 0.0
    if sums is not None:
        total = place * sums[0][3:4] - sums[1]
    if carry is not None:
        shift = jnp.where(lax.broadcasted_iota(jnp.int32, (8, LANES), 0) == 0, ALPHA, 0.0)
        total = total + ((place + shift) * carry[0][3:4] - carry[1])
    return GAIN * total


def chain_forces(tables, weights, steps, emit, group, ahead=1):
    carry = None
    for start in range(0, len(steps), group):
        part = list(enumerate(steps))[start : start + group]
        for index, (own, inner, _) in part:
            put_weights(tables, weights, index, own, own + ahead, inner)
        for index, (own, inner, more) in part:
            if inner:
                sums = own_sums(tables, weights, index, own, own + ahead)
                emit(own, force_of(tables, own, sums, carry))
            carry = next_sums(tables, weights, index, own) if more else None
    return carry


def scratch(rows):
    return pltpu.VMEM((rows, LANES), F32)


VMEM = pl.BlockSpec(memory_space=pltpu.VMEM)
PARAMS = pltpu.CompilerParams(vmem_limit_bytes=48 * 1024 * 1024)


def kick_of(types, mass_ref):
    mass = jnp.zeros(types.shape, F32)
    for kind in range(mass_ref.shape[0]):
        mass = mass + jnp.where(types == kind, mass_ref[kind], 0.0)
    return 0.5 * time_step / mass


def edge_kernel(cells, count_ref, mass_ref, pos_ref, vel_ref, type_ref, out_ref):
    for axis in range(3):
        out_ref[axis * 4 : axis * 4 + 4, :] = pos_ref[axis, 4:8, :]
        out_ref[12 + axis * 3 : 15 + axis * 3, :] = vel_ref[axis, 5:8, :]
    out_ref[21:24, :] = kick_of(type_ref[...], mass_ref)[5:8]
    slot = lax.broadcasted_iota(jnp.int32, (1, LANES), 1)
    for near in range(4):
        occupied = (slot < count_ref[cells - 4 + near]).astype(F32)
        out_ref[24 + near : 25 + near, :] = occupied
    out_ref[28:32, :] = jnp.zeros((4, LANES), F32)


def add_kick(place, speed):
    def emit(slot, force):
        rows = slice(slot * 8, slot * 8 + 8)
        speed[rows, :] = speed[rows, :] + place[rows, :][3:4] * force

    return emit


def first_inner_kernel(
    cells, pos_ref, vel_ref, occ_ref, kick_ref, place, speed, weights, left, right, moved
):
    for axis in range(3):
        place[pl.ds(4 * 8 + axis, cells, stride=8), :] = pos_ref[axis]
        speed[pl.ds(4 * 8 + axis, cells, stride=8), :] = vel_ref[axis]
    place[pl.ds(4 * 8 + 3, cells, stride=8), :] = kick_ref[...]
    tables = (left, right, moved)
    put_tables([pos_ref[axis] for axis in range(3)], occ_ref[...], tables, 4)
    steps = [(own, True, own < cells + 2) for own in range(4, cells + 3)]
    chain_forces(tables, weights, steps, add_kick(place, speed), GROUP)


def first_outer_kernel(
    cells, edge_ref, occ_ref, place_ref, speed_ref, send_ref,
    place, speed, weights, left, right, moved,
):
    half = cells // 4
    place[32:, :] = place_ref[32:, :]
    speed[32:, :] = speed_ref[32:, :]
    for axis in range(3):
        place[pl.ds(axis, 4, stride=8), :] = edge_ref[axis * 4 : axis * 4 + 4, :]
        speed[pl.ds(8 + axis, 3, stride=8), :] = edge_ref[12 + axis * 3 : 15 + axis * 3, :]
    place[pl.ds(8 + 3, 3, stride=8), :] = edge_ref[21:24, :]
    tables = (left, right, moved)
    planes = [place[pl.ds(axis, 8, stride=8), :] for axis in range(3)]
    occupied = jnp.concatenate([edge_ref[24:28, :], occ_ref[0:4, :]], axis=0)
    put_tables(planes, occupied, tables, 0)
    emit = add_kick(place, speed)
    carry = chain_forces(
        tables, weights, [(own, own > 0, True) for own in range(4)], emit, GROUP
    )
    emit(4, force_of(tables, 4, None, carry))
    for kind, source in enumerate((place, speed)):
        for axis in range(3):
            for near in range(4):
                row = (kind * 3 + axis) * 4 + near
                for part in range(2):
                    first = (part * 2 * half + 1 + near) * 8 + axis
                    send_ref[pl.ds(part * WIDE + row, half, stride=2 * WIDE), :] = source[
                        pl.ds(first, half, stride=16), :
                    ]


def cycle(matrix, blocks):
    state = jnp.concatenate(blocks, axis=1)
    high = state.astype(BF16)
    low = (state - high.astype(F32)).astype(BF16)
    return jnp.dot(
        matrix, jnp.concatenate([high, low, high], axis=0), preferred_element_type=F32
    )


def lanes_of(array, index):
    return array[:, index * LANES : (index + 1) * LANES]


def middle_kernel(
    images, matrix_ref, info_ref, got_ref, send_ref, forces, weights, left, right, moved
):
    tables = (left, right, moved)

    def blocks_of(slots):
        return [
            jnp.concatenate(
                [
                    got_ref[pl.ds((kind * 3 + axis) * 4 + slot, images, stride=WIDE), :]
                    for kind in range(2)
                ],
                axis=0,
            )
            for slot in slots
            for axis in range(3)
        ]

    inner = cycle(matrix_ref[...], blocks_of((1, 2)))
    outer = cycle(matrix_ref[:images, :], blocks_of((0, 3)))
    for slot in range(4):
        source, first = ((outer, 0), (inner, 0), (inner, 3), (outer, 3))[slot]
        planes = [lanes_of(source, first + axis)[:images] for axis in range(3)]
        occupied = jnp.broadcast_to(info_ref[slot : slot + 1, :], (images, LANES))
        put_tables(planes, occupied, tables, slot * images, ("lr", "lrm", "lrm", "m")[slot])

    def emit(cell, force):
        row = (cell - images) * 8
        forces[row : row + 8, :] = force

    steps = [
        (slot * images + image, slot > 0, slot < 2)
        for image in range(images)
        for slot in range(3)
    ]
    chain_forces(tables, weights, steps, emit, 12, ahead=images)
    blocks = []
    for parity in range(2):
        kick = 2.0 * info_ref[4 + parity : 5 + parity, :]
        for axis in range(3):
            now = lanes_of(inner, parity * 3 + axis)
            force = forces[pl.ds(parity * images * 8 + axis, images, stride=8), :]
            blocks.append(jnp.concatenate([now[:images], now[images:] + kick * force], axis=0))
    ahead = cycle(matrix_ref[...], blocks)
    for parity in range(2):
        for axis in range(3):
            after = lanes_of(ahead, parity * 3 + axis)
            for kind in range(2):
                row = (kind * 3 + axis) * 2 + parity
                send_ref[pl.ds(row, images, stride=SPAN), :] = after[
                    kind * images : (kind + 1) * images
                ]


def last_inner_kernel(
    cells, got_ref, first_ref, occ_ref, kick_ref, place, speed,
    occ_all, weights, left, right, moved,
):
    half = cells // 4
    for kind, target in enumerate((place, speed)):
        for axis in range(3):
            for parity in range(2):
                row = (kind * 3 + axis) * 2 + parity
                for part in range(2):
                    first = (part * 2 * half + parity) * 8 + axis
                    target[pl.ds(first, half, stride=16), :] = got_ref[
                        pl.ds(part * SPAN + row, half, stride=2 * SPAN), :
                    ]
    place[pl.ds(2 * 8 + 3, cells, stride=8), :] = kick_ref[...]
    occ_all[0:2, :] = first_ref[26:28, :]
    occ_all[2:cells, :] = occ_ref[: cells - 2, :]
    tables = (left, right, moved)
    planes = [place[pl.ds(axis, cells, stride=8), :] for axis in range(3)]
    put_tables(planes, occ_all[...], tables, 0)
    emit = add_kick(place, speed)
    steps = [(own, own > 1, True) for own in range(1, cells - 1)]
    carry = chain_forces(tables, weights, steps, emit, GROUP)
    emit(cells - 1, force_of(tables, cells - 1, None, carry))


def last_outer_kernel(
    cells, edge_ref, occ_ref, place_ref, speed_ref, pos_ref, vel_ref,
    place, speed, weights, left, right, moved,
):
    base = cells - 8
    place[0:64, :] = place_ref[base * 8 : cells * 8, :]
    speed[0:64, :] = speed_ref[base * 8 : cells * 8, :]
    for axis in range(3):
        for parity in range(2):
            slot = (8 + parity) * 8 + axis
            row = axis * 2 + parity
            place[slot : slot + 1, :] = edge_ref[row : row + 1, :]
            speed[slot : slot + 1, :] = edge_ref[row + 6 : row + 7, :]
        slot = 10 * 8 + axis
        place[slot : slot + 1, :] = edge_ref[12 + axis : 13 + axis, :]
    for parity in range(2):
        slot = (8 + parity) * 8 + 3
        place[slot : slot + 1, :] = place_ref[
            (cells + parity) * 8 + 3 : (cells + parity) * 8 + 4, :
        ]
    tables = (left, right, moved)
    planes = [place[pl.ds(axis, 16, stride=8), :] for axis in range(3)]
    occupied = jnp.concatenate(
        [
            jnp.zeros((7, LANES), F32),
            occ_ref[cells - 3 : cells, :],
            edge_ref[15:16, :],
            jnp.zeros((5, LANES), F32),
        ],
        axis=0,
    )
    put_tables(planes, occupied, tables, 0)
    steps = [(own, True, own < 9) for own in range(7, 10)]
    chain_forces(tables, weights, steps, add_kick(place, speed), GROUP)
    for axis in range(3):
        for out_ref, whole, end in ((pos_ref, place_ref, place), (vel_ref, speed_ref, speed)):
            out_ref[axis, 0 : base, :] = whole[pl.ds(2 * 8 + axis, base, stride=8), :]
            out_ref[axis, base:cells, :] = end[pl.ds(2 * 8 + axis, 8, stride=8), :]


def local(positions, velocities, counts, types, masses):
    images = lax.axis_size("image")
    slabs = lax.axis_size("space")
    cells = positions.shape[1]
    rows = cells + 8

    def slab_shift(array, distance):
        pairs = [(s, (s + distance) % slabs) for s in range(slabs)]
        return lax.ppermute(array, "space", pairs)

    def transpose(array):
        blocks = array.reshape(images, array.shape[0] // images // 4, 4, LANES)
        blocks = lax.all_to_all(blocks, "image", split_axis=0, concat_axis=0, tiled=True)
        return blocks.reshape(array.shape)

    def call(kernel, outs, scratches, *args):
        return pl.pallas_call(
            kernel,
            out_shape=outs,
            in_specs=[VMEM] * len(args),
            out_specs=jax.tree.map(lambda _: VMEM, outs),
            scratch_shapes=scratches,
            compiler_params=PARAMS,
            cost_estimate=pl.CostEstimate(
                flops=20_000_000_000, bytes_accessed=1_000_000, transcendentals=0
            ),
        )(*args)

    def shaped(*shape):
        return jax.ShapeDtypeStruct(shape, F32)

    def weight_scratch(steps):
        return pltpu.VMEM((steps * LANES, 2 * LANES), BF16)

    slot_index = lax.broadcasted_iota(jnp.int32, types.shape, 1)
    occupied = (slot_index < counts[:, None]).astype(F32)
    type_index = lax.broadcasted_iota(jnp.int32, (masses.shape[0],) + types.shape, 0)
    chosen = jnp.sum(jnp.where(types[None] == type_index, masses[:, None, None], 0.0), axis=0)
    kick = 0.5 * time_step * (1.0 / chosen)
    matrix = jnp.asarray(cycle_matrix(images))
    group = lax.axis_index("image")
    block = (group % 2) * (images // 2) + group // 2

    pos = positions[0].transpose(1, 0, 2)
    vel = velocities[0].transpose(1, 0, 2)
    window = shaped(rows * 8, LANES)
    slab_scratch = [weight_scratch(cells)] + [scratch(rows * ROWS)] * 3
    edge_scratch = [scratch(rows * 8)] * 2 + [weight_scratch(8)] + [scratch(16 * ROWS)] * 3
    last = cells // 8 - 1
    smem = pl.BlockSpec(memory_space=pltpu.SMEM)
    edge = pl.pallas_call(
        lambda *r: edge_kernel(cells, *r),
        grid=(1,),
        out_shape=shaped(32, LANES),
        in_specs=[
            smem,
            smem,
            pl.BlockSpec((3, 8, LANES), lambda i: (0, last, 0)),
            pl.BlockSpec((3, 8, LANES), lambda i: (0, last, 0)),
            pl.BlockSpec((8, LANES), lambda i: (last, 0)),
        ],
        out_specs=pl.BlockSpec((32, LANES), lambda i: (0, 0)),
        compiler_params=pltpu.CompilerParams(vmem_limit_bytes=62 * 1024 * 1024),
    )(counts, masses, pos, vel, types)
    edge = slab_shift(edge, 1)
    place, speed = call(
        lambda *r: first_inner_kernel(cells, *r),
        (window, window),
        slab_scratch,
        pos, vel, occupied, kick,
    )
    send = call(
        lambda *r: first_outer_kernel(cells, *r),
        shaped(images * WIDE, LANES),
        edge_scratch,
        edge, occupied, place, speed,
    )
    got = transpose(send)
    occ_wide = jnp.concatenate([edge[24:28], occupied], axis=0)
    kick_wide = jnp.concatenate([edge[21:24], kick], axis=0)
    info = jnp.concatenate(
        [
            lax.dynamic_slice_in_dim(occ_wide, 2 * block + 1, 4, 0),
            lax.dynamic_slice_in_dim(kick_wide, 2 * block + 1, 2, 0),
            occupied[0:1],
            jnp.zeros((1, LANES), F32),
        ],
        axis=0,
    )
    send = call(
        lambda *r: middle_kernel(images, *r),
        shaped(images * SPAN, LANES),
        [scratch(2 * images * 8), weight_scratch(3 * images)] + [scratch(4 * images * ROWS)] * 3,
        matrix, info, got,
    )
    got = transpose(send)
    chunk = 2 * SPAN
    message = jnp.concatenate(
        [got[0:SPAN]]
        + [got[chunk + 2 * axis : chunk + 2 * axis + 1] for axis in range(3)]
        + [info[6:7]],
        axis=0,
    )
    message = slab_shift(message, -1)
    place, speed = call(
        lambda *r: last_inner_kernel(cells, *r),
        (window, window),
        [scratch(cells)] + slab_scratch,
        got, edge, occupied, kick,
    )
    pos, vel = call(
        lambda *r: last_outer_kernel(cells, *r),
        (shaped(*pos.shape), shaped(*vel.shape)),
        edge_scratch,
        message, occupied, place, speed,
    )
    return pos.transpose(1, 0, 2)[None], vel.transpose(1, 0, 2)[None]


def solution(mesh):
    return jax.shard_map(
        local,
        mesh=mesh,
        in_specs=(
            P("image", "space", None, None),
            P("image", "space", None, None),
            P("space"),
            P("space", None),
            P(),
        ),
        out_specs=(P("image", "space", None, None), P("image", "space", None, None)),
        check_vma=False,
    )
```

```python
import math

import jax
import jax.numpy as jnp
import ml_dtypes
import numpy as np
from jax import lax
from jax.experimental import pallas as pl
from jax.experimental.pallas import tpu as pltpu
from jax.sharding import PartitionSpec as P

STEPS = 2

time_step = 1.5
cycle_omega = 6.0
strength = 0.01
width_sq = 0.25

F32 = jnp.float32
BF16 = jnp.bfloat16
LANES = 128
ROWS = 24
SPAN = 12
GROUP = 13
WIDE = 24
ALPHA = math.sqrt(math.log2(math.e) / width_sq)
GAIN = strength / width_sq / ALPHA
FAR = 1e12


def cycle_matrix(count):
    j = np.arange(count, dtype=np.float64)[:, None]
    k = np.arange(count, dtype=np.float64)[None, :]
    half = count // 2
    phase = 2.0 * np.pi * j * k / count
    table = np.where(
        k < half, np.sqrt(2.0 / count) * np.cos(phase), np.sqrt(2.0 / count) * np.sin(phase)
    )
    table = np.where(k == 0, 1.0 / np.sqrt(count), table)
    table = np.where(k == half, np.cos(np.pi * j) / np.sqrt(count), table)
    omega = 2.0 * cycle_omega * np.sin(np.pi * k[0] / count)
    angle = omega * time_step
    to_position = np.where(k[0] == 0, time_step, np.sin(angle) / np.where(k[0] == 0, 1.0, omega))
    same = (table * np.cos(angle)) @ table.T
    from_velocity = (table * to_position) @ table.T
    from_position = (table * (-omega * np.sin(angle))) @ table.T
    matrix = np.block([[same, from_velocity], [from_position, same]])
    high = matrix.astype(ml_dtypes.bfloat16)
    low = (matrix - high.astype(np.float64)).astype(ml_dtypes.bfloat16)
    return np.concatenate([high, high, low], axis=1)


def split3(value):
    high = value.astype(BF16).astype(F32)
    rest = value - high
    mid = rest.astype(BF16).astype(F32)
    low = (rest - mid).astype(BF16).astype(F32)
    return high, mid, low


def put_tables(planes, occupied, tables, start, sides="lrm"):
    left, right, moved = tables
    count = planes[0].shape[0]
    one = jnp.ones_like(planes[0])

    def put(ref, row, value):
        ref[pl.ds(start * ROWS + row, count, stride=ROWS), :] = value

    def norm(parts):
        total = parts[0] * parts[0] + parts[1] * parts[1] + parts[2] * parts[2]
        return split3(-0.5 * total - FAR * (1.0 - occupied))

    def put_right(ref, pieces, norms):
        for axis in range(3):
            high, mid, low = pieces[axis]
            for row, value in ((0, high), (4, high), (8, mid), (12, high), (16, low), (20, mid)):
                put(ref, row + axis, value)
        for piece in range(3):
            put(ref, 8 * piece + 3, one)
            put(ref, 8 * piece + 7, norms[piece])

    scaled = [ALPHA * plane for plane in planes]
    pieces = [split3(part) for part in scaled]
    if "l" in sides:
        norms = norm(scaled)
        for axis in range(3):
            high, mid, low = pieces[axis]
            for row, value in ((0, high), (4, mid), (8, high), (12, low), (16, high), (20, mid)):
                put(left, row + axis, value)
        for piece in range(3):
            put(left, 8 * piece + 3, norms[piece])
            put(left, 8 * piece + 7, one)
        put_right(right, pieces, norms)
    if "m" in sides:
        ahead = ALPHA * (planes[0] + 1.0)
        put_right(moved, [split3(ahead)] + pieces[1:], norm([ahead, scaled[1], scaled[2]]))


def table_rows(ref, cell):
    return ref[cell * ROWS : (cell + 1) * ROWS, :]


def factor(table):
    pad = jnp.zeros((8, LANES), F32)
    return jnp.concatenate([table, pad], axis=0).astype(BF16)


def put_weights(tables, weights, index, own, near, full):
    left, right, moved = tables
    others = factor(table_rows(moved, near))
    if full:
        others = jnp.concatenate([factor(table_rows(right, own)), others], axis=1)
    exponent = lax.dot_general(
        factor(table_rows(left, own)),
        others,
        (((0,), (0,)), ((), ())),
        preferred_element_type=F32,
    )
    start = 0 if full else LANES
    weights[index * LANES : (index + 1) * LANES, start:] = jnp.exp2(exponent).astype(BF16)


def fold(sums):
    return sums[0:8], sums[0:8] + sums[8:16] + sums[16:24]


def own_sums(tables, weights, index, own, near):
    both = jnp.concatenate(
        [factor(table_rows(tables[1], own)), factor(table_rows(tables[2], near))], axis=1
    )
    weight = weights[index * LANES : (index + 1) * LANES, :]
    return fold(
        lax.dot_general(both, weight, (((1,), (1,)), ((), ())), preferred_element_type=F32)
    )


def next_sums(tables, weights, index, own):
    weight = weights[index * LANES : (index + 1) * LANES, LANES:]
    return fold(
        lax.dot_general(
            factor(table_rows(tables[1], own)),
            weight,
            (((1,), (0,)), ((), ())),
            preferred_element_type=F32,
        )
    )


def force_of(tables, own, sums, carry):
    table = table_rows(tables[1], own)
    place = table[0:8] + table[8:16] + table[16:24]
    total = 0.0
    if sums is not None:
        total = place * sums[0][3:4] - sums[1]
    if carry is not None:
        shift = jnp.where(lax.broadcasted_iota(jnp.int32, (8, LANES), 0) == 0, ALPHA, 0.0)
        total = total + ((place + shift) * carry[0][3:4] - carry[1])
    return GAIN * total


def chain_forces(tables, weights, steps, emit, group, ahead=1):
    carry = None
    for start in range(0, len(steps), group):
        part = list(enumerate(steps))[start : start + group]
        for index, (own, inner, _) in part:
            put_weights(tables, weights, index, own, own + ahead, inner)
        for index, (own, inner, more) in part:
            if inner:
                sums = own_sums(tables, weights, index, own, own + ahead)
                emit(own, force_of(tables, own, sums, carry))
            carry = next_sums(tables, weights, index, own) if more else None
    return carry


def scratch(rows):
    return pltpu.VMEM((rows, LANES), F32)


VMEM = pl.BlockSpec(memory_space=pltpu.VMEM)
SMEM = pl.BlockSpec(memory_space=pltpu.SMEM)
PARAMS = pltpu.CompilerParams(vmem_limit_bytes=48 * 1024 * 1024)


def kick_of(types, mass_ref):
    mass = jnp.zeros(types.shape, F32)
    for kind in range(mass_ref.shape[0]):
        mass = mass + jnp.where(types == kind, mass_ref[kind], 0.0)
    return 0.5 * time_step / mass


def edge_kernel(cells, count_ref, mass_ref, pos_ref, vel_ref, type_ref, out_ref):
    for axis in range(3):
        out_ref[axis * 4 : axis * 4 + 4, :] = pos_ref[axis, 4:8, :]
        out_ref[12 + axis * 3 : 15 + axis * 3, :] = vel_ref[axis, 5:8, :]
    out_ref[21:24, :] = kick_of(type_ref[...], mass_ref)[5:8]
    slot = lax.broadcasted_iota(jnp.int32, (1, LANES), 1)
    for near in range(4):
        occupied = (slot < count_ref[cells - 4 + near]).astype(F32)
        out_ref[24 + near : 25 + near, :] = occupied
    out_ref[28:32, :] = jnp.zeros((4, LANES), F32)


def add_kick(place, speed):
    def emit(slot, force):
        rows = slice(slot * 8, slot * 8 + 8)
        speed[rows, :] = speed[rows, :] + place[rows, :][3:4] * force

    return emit


def first_inner_kernel(
    cells, pos_ref, vel_ref, occ_ref, kick_ref, place, speed, weights, left, right, moved
):
    for axis in range(3):
        place[pl.ds(4 * 8 + axis, cells, stride=8), :] = pos_ref[axis]
        speed[pl.ds(4 * 8 + axis, cells, stride=8), :] = vel_ref[axis]
    place[pl.ds(4 * 8 + 3, cells, stride=8), :] = kick_ref[...]
    tables = (left, right, moved)
    put_tables([pos_ref[axis] for axis in range(3)], occ_ref[...], tables, 4)
    steps = [(own, True, own < cells + 2) for own in range(4, cells + 3)]
    chain_forces(tables, weights, steps, add_kick(place, speed), GROUP)


def first_outer_kernel(
    cells, block_ref, edge_ref, occ_ref, kick_ref, place_ref, speed_ref, send_ref, info_ref,
    occ_all, kick_all, place, speed, weights, left, right, moved,
):
    half = cells // 4
    place[32:, :] = place_ref[32:, :]
    speed[32:, :] = speed_ref[32:, :]
    for axis in range(3):
        place[pl.ds(axis, 4, stride=8), :] = edge_ref[axis * 4 : axis * 4 + 4, :]
        speed[pl.ds(8 + axis, 3, stride=8), :] = edge_ref[12 + axis * 3 : 15 + axis * 3, :]
    place[pl.ds(8 + 3, 3, stride=8), :] = edge_ref[21:24, :]
    tables = (left, right, moved)
    planes = [place[pl.ds(axis, 8, stride=8), :] for axis in range(3)]
    occupied = jnp.concatenate([edge_ref[24:28, :], occ_ref[0:4, :]], axis=0)
    put_tables(planes, occupied, tables, 0)
    emit = add_kick(place, speed)
    carry = chain_forces(
        tables, weights, [(own, own > 0, True) for own in range(4)], emit, GROUP
    )
    emit(4, force_of(tables, 4, None, carry))
    occ_all[0:4, :] = edge_ref[24:28, :]
    occ_all[4 : cells + 4, :] = occ_ref[...]
    kick_all[0:3, :] = edge_ref[21:24, :]
    kick_all[3 : cells + 3, :] = kick_ref[...]
    start = 2 * block_ref[0] + 1
    for near in range(4):
        info_ref[near : near + 1, :] = occ_all[pl.ds(start + near, 1), :]
    for near in range(2):
        info_ref[4 + near : 5 + near, :] = kick_all[pl.ds(start + near, 1), :]
    info_ref[6:7, :] = occ_ref[0:1, :]
    info_ref[7:8, :] = jnp.zeros((1, LANES), F32)
    for kind, source in enumerate((place, speed)):
        for axis in range(3):
            for near in range(4):
                row = (kind * 3 + axis) * 4 + near
                for part in range(2):
                    first = (part * 2 * half + 1 + near) * 8 + axis
                    send_ref[pl.ds(part * WIDE + row, half, stride=2 * WIDE), :] = source[
                        pl.ds(first, half, stride=16), :
                    ]


def cycle(matrix, blocks):
    state = jnp.concatenate(blocks, axis=1)
    high = state.astype(BF16)
    low = (state - high.astype(F32)).astype(BF16)
    return jnp.dot(
        matrix, jnp.concatenate([high, low, high], axis=0), preferred_element_type=F32
    )


def lanes_of(array, index):
    return array[:, index * LANES : (index + 1) * LANES]


def middle_kernel(
    images, matrix_ref, info_ref, got_ref, send_ref, forces, weights, left, right, moved
):
    tables = (left, right, moved)

    def blocks_of(slots):
        return [
            jnp.concatenate(
                [
                    got_ref[pl.ds((kind * 3 + axis) * 4 + slot, images, stride=WIDE), :]
                    for kind in range(2)
                ],
                axis=0,
            )
            for slot in slots
            for axis in range(3)
        ]

    inner = cycle(matrix_ref[...], blocks_of((1, 2)))
    outer = cycle(matrix_ref[:images, :], blocks_of((0, 3)))
    for slot in range(4):
        source, first = ((outer, 0), (inner, 0), (inner, 3), (outer, 3))[slot]
        planes = [lanes_of(source, first + axis)[:images] for axis in range(3)]
        occupied = jnp.broadcast_to(info_ref[slot : slot + 1, :], (images, LANES))
        put_tables(planes, occupied, tables, slot * images, ("lr", "lrm", "lrm", "m")[slot])

    def emit(cell, force):
        row = (cell - images) * 8
        forces[row : row + 8, :] = force

    steps = [
        (slot * images + image, slot > 0, slot < 2)
        for image in range(images)
        for slot in range(3)
    ]
    chain_forces(tables, weights, steps, emit, 12, ahead=images)
    blocks = []
    for parity in range(2):
        kick = 2.0 * info_ref[4 + parity : 5 + parity, :]
        for axis in range(3):
            now = lanes_of(inner, parity * 3 + axis)
            force = forces[pl.ds(parity * images * 8 + axis, images, stride=8), :]
            blocks.append(jnp.concatenate([now[:images], now[images:] + kick * force], axis=0))
    ahead = cycle(matrix_ref[...], blocks)
    for parity in range(2):
        for axis in range(3):
            after = lanes_of(ahead, parity * 3 + axis)
            for kind in range(2):
                row = (kind * 3 + axis) * 2 + parity
                send_ref[pl.ds(row, images, stride=SPAN), :] = after[
                    kind * images : (kind + 1) * images
                ]


def last_inner_kernel(
    cells, got_ref, first_ref, occ_ref, kick_ref, place, speed,
    occ_all, weights, left, right, moved,
):
    half = cells // 4
    for kind, target in enumerate((place, speed)):
        for axis in range(3):
            for parity in range(2):
                row = (kind * 3 + axis) * 2 + parity
                for part in range(2):
                    first = (part * 2 * half + parity) * 8 + axis
                    target[pl.ds(first, half, stride=16), :] = got_ref[
                        pl.ds(part * SPAN + row, half, stride=2 * SPAN), :
                    ]
    place[pl.ds(2 * 8 + 3, cells, stride=8), :] = kick_ref[...]
    occ_all[0:2, :] = first_ref[26:28, :]
    occ_all[2:cells, :] = occ_ref[: cells - 2, :]
    tables = (left, right, moved)
    planes = [place[pl.ds(axis, cells, stride=8), :] for axis in range(3)]
    put_tables(planes, occ_all[...], tables, 0)
    emit = add_kick(place, speed)
    steps = [(own, own > 1, True) for own in range(1, cells - 1)]
    carry = chain_forces(tables, weights, steps, emit, GROUP)
    emit(cells - 1, force_of(tables, cells - 1, None, carry))


def last_outer_kernel(
    cells, edge_ref, occ_ref, place_ref, speed_ref, pos_ref, vel_ref,
    place, speed, weights, left, right, moved,
):
    base = cells - 8
    place[0:64, :] = place_ref[base * 8 : cells * 8, :]
    speed[0:64, :] = speed_ref[base * 8 : cells * 8, :]
    for axis in range(3):
        for parity in range(2):
            slot = (8 + parity) * 8 + axis
            row = axis * 2 + parity
            place[slot : slot + 1, :] = edge_ref[row : row + 1, :]
            speed[slot : slot + 1, :] = edge_ref[row + 6 : row + 7, :]
        slot = 10 * 8 + axis
        place[slot : slot + 1, :] = edge_ref[12 + axis : 13 + axis, :]
    for parity in range(2):
        slot = (8 + parity) * 8 + 3
        place[slot : slot + 1, :] = place_ref[
            (cells + parity) * 8 + 3 : (cells + parity) * 8 + 4, :
        ]
    tables = (left, right, moved)
    planes = [place[pl.ds(axis, 16, stride=8), :] for axis in range(3)]
    occupied = jnp.concatenate(
        [
            jnp.zeros((7, LANES), F32),
            occ_ref[cells - 3 : cells, :],
            edge_ref[15:16, :],
            jnp.zeros((5, LANES), F32),
        ],
        axis=0,
    )
    put_tables(planes, occupied, tables, 0)
    steps = [(own, True, own < 9) for own in range(7, 10)]
    chain_forces(tables, weights, steps, add_kick(place, speed), GROUP)
    for axis in range(3):
        for out_ref, whole, end in ((pos_ref, place_ref, place), (vel_ref, speed_ref, speed)):
            out_ref[axis, 0 : base, :] = whole[pl.ds(2 * 8 + axis, base, stride=8), :]
            out_ref[axis, base:cells, :] = end[pl.ds(2 * 8 + axis, 8, stride=8), :]


def local(positions, velocities, counts, types, masses):
    images = lax.axis_size("image")
    slabs = lax.axis_size("space")
    cells = positions.shape[1]
    rows = cells + 8

    def slab_shift(array, distance):
        pairs = [(s, (s + distance) % slabs) for s in range(slabs)]
        return lax.ppermute(array, "space", pairs)

    def transpose(array):
        blocks = array.reshape(images, array.shape[0] // images // 4, 4, LANES)
        blocks = lax.all_to_all(blocks, "image", split_axis=0, concat_axis=0, tiled=True)
        return blocks.reshape(array.shape)

    def call(kernel, outs, scratches, *args):
        return pl.pallas_call(
            kernel,
            out_shape=outs,
            in_specs=[SMEM if arg.ndim == 1 else VMEM for arg in args],
            out_specs=jax.tree.map(lambda _: VMEM, outs),
            scratch_shapes=scratches,
            compiler_params=PARAMS,
            cost_estimate=pl.CostEstimate(
                flops=20_000_000_000, bytes_accessed=1_000_000, transcendentals=0
            ),
        )(*args)

    def shaped(*shape):
        return jax.ShapeDtypeStruct(shape, F32)

    def weight_scratch(steps):
        return pltpu.VMEM((steps * LANES, 2 * LANES), BF16)

    slot_index = lax.broadcasted_iota(jnp.int32, types.shape, 1)
    occupied = (slot_index < counts[:, None]).astype(F32)
    type_index = lax.broadcasted_iota(jnp.int32, (masses.shape[0],) + types.shape, 0)
    chosen = jnp.sum(jnp.where(types[None] == type_index, masses[:, None, None], 0.0), axis=0)
    kick = 0.5 * time_step * (1.0 / chosen)
    matrix = jnp.asarray(cycle_matrix(images))
    group = lax.axis_index("image")
    block = (group % 2) * (images // 2) + group // 2

    pos = positions[0].transpose(1, 0, 2)
    vel = velocities[0].transpose(1, 0, 2)
    window = shaped(rows * 8, LANES)
    slab_scratch = [weight_scratch(cells)] + [scratch(rows * ROWS)] * 3
    edge_scratch = [scratch(rows * 8)] * 2 + [weight_scratch(8)] + [scratch(16 * ROWS)] * 3
    last = cells // 8 - 1
    edge = pl.pallas_call(
        lambda *r: edge_kernel(cells, *r),
        grid=(1,),
        out_shape=shaped(32, LANES),
        in_specs=[
            SMEM,
            SMEM,
            pl.BlockSpec((3, 8, LANES), lambda i: (0, last, 0)),
            pl.BlockSpec((3, 8, LANES), lambda i: (0, last, 0)),
            pl.BlockSpec((8, LANES), lambda i: (last, 0)),
        ],
        out_specs=pl.BlockSpec((32, LANES), lambda i: (0, 0)),
        compiler_params=pltpu.CompilerParams(vmem_limit_bytes=62 * 1024 * 1024),
    )(counts, masses, pos, vel, types)
    edge = slab_shift(edge, 1)
    place, speed = call(
        lambda *r: first_inner_kernel(cells, *r),
        (window, window),
        slab_scratch,
        pos, vel, occupied, kick,
    )
    send, info = call(
        lambda *r: first_outer_kernel(cells, *r),
        (shaped(images * WIDE, LANES), shaped(8, LANES)),
        [scratch(rows)] * 2 + edge_scratch,
        block.reshape(1), edge, occupied, kick, place, speed,
    )
    got = transpose(send)
    send = call(
        lambda *r: middle_kernel(images, *r),
        shaped(images * SPAN, LANES),
        [scratch(2 * images * 8), weight_scratch(3 * images)] + [scratch(4 * images * ROWS)] * 3,
        matrix, info, got,
    )
    got, info = lax.optimization_barrier((transpose(send), info))
    chunk = 2 * SPAN
    message = jnp.concatenate(
        [got[0:SPAN]]
        + [got[chunk + 2 * axis : chunk + 2 * axis + 1] for axis in range(3)]
        + [info[6:7]],
        axis=0,
    )
    message = slab_shift(message, -1)
    place, speed = call(
        lambda *r: last_inner_kernel(cells, *r),
        (window, window),
        [scratch(cells)] + slab_scratch,
        got, edge, occupied, kick,
    )
    pos, vel = call(
        lambda *r: last_outer_kernel(cells, *r),
        (shaped(*pos.shape), shaped(*vel.shape)),
        edge_scratch,
        message, occupied, place, speed,
    )
    return pos.transpose(1, 0, 2)[None], vel.transpose(1, 0, 2)[None]


def solution(mesh):
    return jax.shard_map(
        local,
        mesh=mesh,
        in_specs=(
            P("image", "space", None, None),
            P("image", "space", None, None),
            P("space"),
            P("space", None),
            P(),
        ),
        out_specs=(P("image", "space", None, None), P("image", "space", None, None)),
        check_vma=False,
    )
```

```python
import math

import jax
import jax.numpy as jnp
import ml_dtypes
import numpy as np
from jax import lax
from jax.experimental import pallas as pl
from jax.experimental.pallas import tpu as pltpu
from jax.sharding import PartitionSpec as P

STEPS = 2

time_step = 1.5
cycle_omega = 6.0
strength = 0.01
width_sq = 0.25

F32 = jnp.float32
BF16 = jnp.bfloat16
LANES = 128
ROWS = 24
SPAN = 12
GROUP = 13
WIDE = 24
ALPHA = math.sqrt(math.log2(math.e) / width_sq)
GAIN = strength / width_sq / ALPHA
FAR = 1e12


def cycle_matrix(count):
    j = np.arange(count, dtype=np.float64)[:, None]
    k = np.arange(count, dtype=np.float64)[None, :]
    half = count // 2
    phase = 2.0 * np.pi * j * k / count
    table = np.where(
        k < half, np.sqrt(2.0 / count) * np.cos(phase), np.sqrt(2.0 / count) * np.sin(phase)
    )
    table = np.where(k == 0, 1.0 / np.sqrt(count), table)
    table = np.where(k == half, np.cos(np.pi * j) / np.sqrt(count), table)
    omega = 2.0 * cycle_omega * np.sin(np.pi * k[0] / count)
    angle = omega * time_step
    to_position = np.where(k[0] == 0, time_step, np.sin(angle) / np.where(k[0] == 0, 1.0, omega))
    same = (table * np.cos(angle)) @ table.T
    from_velocity = (table * to_position) @ table.T
    from_position = (table * (-omega * np.sin(angle))) @ table.T
    matrix = np.block([[same, from_velocity], [from_position, same]])
    high = matrix.astype(ml_dtypes.bfloat16)
    low = (matrix - high.astype(np.float64)).astype(ml_dtypes.bfloat16)
    return np.concatenate([high, high, low], axis=1)


def split3(value):
    high = value.astype(BF16).astype(F32)
    rest = value - high
    mid = rest.astype(BF16).astype(F32)
    low = (rest - mid).astype(BF16).astype(F32)
    return high, mid, low


def put_tables(planes, occupied, tables, start, sides="lrm"):
    left, right, moved = tables
    count = planes[0].shape[0]
    one = jnp.ones_like(planes[0])

    def put(ref, row, value):
        ref[pl.ds(start * ROWS + row, count, stride=ROWS), :] = value

    def norm(parts):
        total = parts[0] * parts[0] + parts[1] * parts[1] + parts[2] * parts[2]
        return split3(-0.5 * total - FAR * (1.0 - occupied))

    def put_right(ref, pieces, norms):
        for axis in range(3):
            high, mid, low = pieces[axis]
            for row, value in ((0, high), (4, low), (8, mid), (12, high), (16, high), (20, mid)):
                put(ref, row + axis, value)
        for piece in range(3):
            put(ref, 8 * piece + 3, one)
            put(ref, 8 * piece + 7, norms[piece])

    scaled = [ALPHA * plane for plane in planes]
    pieces = [split3(part) for part in scaled]
    if "l" in sides:
        norms = norm(scaled)
        for axis in range(3):
            high, mid, low = pieces[axis]
            for row, value in ((0, high), (4, high), (8, high), (12, mid), (16, low), (20, mid)):
                put(left, row + axis, value)
        for piece in range(3):
            put(left, 8 * piece + 3, norms[piece])
            put(left, 8 * piece + 7, one)
        put_right(right, pieces, norms)
    if "m" in sides:
        ahead = ALPHA * (planes[0] + 1.0)
        put_right(moved, [split3(ahead)] + pieces[1:], norm([ahead, scaled[1], scaled[2]]))


def table_rows(ref, cell):
    return ref[cell * ROWS : (cell + 1) * ROWS, :]


def factor(table):
    pad = jnp.zeros((8, LANES), F32)
    return jnp.concatenate([table, pad], axis=0).astype(BF16)


def put_weights(tables, weights, index, own, near, full):
    left, right, moved = tables
    others = factor(table_rows(moved, near))
    if full:
        others = jnp.concatenate([factor(table_rows(right, own)), others], axis=1)
    exponent = lax.dot_general(
        factor(table_rows(left, own)),
        others,
        (((0,), (0,)), ((), ())),
        preferred_element_type=F32,
    )
    start = 0 if full else LANES
    weights[index * LANES : (index + 1) * LANES, start:] = jnp.exp2(exponent).astype(BF16)


def fold(rows):
    return rows[0:8], rows[0:8] + rows[8:16] + pltpu.roll(rows[0:8], 4, 0)


def pieces_of(table):
    return table[0:16].astype(BF16)


def own_sums(tables, weights, index, own, near):
    both = jnp.concatenate(
        [pieces_of(table_rows(tables[1], own)), pieces_of(table_rows(tables[2], near))], axis=1
    )
    weight = weights[index * LANES : (index + 1) * LANES, :]
    return fold(
        lax.dot_general(both, weight, (((1,), (1,)), ((), ())), preferred_element_type=F32)
    )


def next_sums(tables, weights, index, own):
    weight = weights[index * LANES : (index + 1) * LANES, LANES:]
    return fold(
        lax.dot_general(
            pieces_of(table_rows(tables[1], own)),
            weight,
            (((1,), (0,)), ((), ())),
            preferred_element_type=F32,
        )
    )


def force_of(tables, own, sums, carry):
    place = fold(table_rows(tables[1], own))[1]
    total = 0.0
    if sums is not None:
        total = place * sums[0][3:4] - sums[1]
    if carry is not None:
        shift = jnp.where(lax.broadcasted_iota(jnp.int32, (8, LANES), 0) == 0, ALPHA, 0.0)
        total = total + ((place + shift) * carry[0][3:4] - carry[1])
    return GAIN * total


def chain_forces(tables, weights, steps, emit, group, ahead=1):
    carry = None
    for start in range(0, len(steps), group):
        part = list(enumerate(steps))[start : start + group]
        for index, (own, inner, _) in part:
            put_weights(tables, weights, index, own, own + ahead, inner)
        for index, (own, inner, more) in part:
            if inner:
                sums = own_sums(tables, weights, index, own, own + ahead)
                emit(own, force_of(tables, own, sums, carry))
            carry = next_sums(tables, weights, index, own) if more else None
    return carry


def scratch(rows):
    return pltpu.VMEM((rows, LANES), F32)


VMEM = pl.BlockSpec(memory_space=pltpu.VMEM)
SMEM = pl.BlockSpec(memory_space=pltpu.SMEM)
PARAMS = pltpu.CompilerParams(vmem_limit_bytes=48 * 1024 * 1024)


def kick_of(types, mass_ref):
    mass = jnp.zeros(types.shape, F32)
    for kind in range(mass_ref.shape[0]):
        mass = mass + jnp.where(types == kind, mass_ref[kind], 0.0)
    return 0.5 * time_step / mass


def edge_kernel(cells, count_ref, mass_ref, pos_ref, vel_ref, type_ref, out_ref):
    for axis in range(3):
        out_ref[axis * 4 : axis * 4 + 4, :] = pos_ref[axis, 4:8, :]
        out_ref[12 + axis * 3 : 15 + axis * 3, :] = vel_ref[axis, 5:8, :]
    out_ref[21:24, :] = kick_of(type_ref[...], mass_ref)[5:8]
    slot = lax.broadcasted_iota(jnp.int32, (1, LANES), 1)
    for near in range(4):
        occupied = (slot < count_ref[cells - 4 + near]).astype(F32)
        out_ref[24 + near : 25 + near, :] = occupied
    out_ref[28:32, :] = jnp.zeros((4, LANES), F32)


def add_kick(place, speed):
    def emit(slot, force):
        rows = slice(slot * 8, slot * 8 + 8)
        speed[rows, :] = speed[rows, :] + place[rows, :][3:4] * force

    return emit


def first_inner_kernel(
    cells, pos_ref, vel_ref, occ_ref, kick_ref, place, speed, weights, left, right, moved
):
    for axis in range(3):
        place[pl.ds(4 * 8 + axis, cells, stride=8), :] = pos_ref[axis]
        speed[pl.ds(4 * 8 + axis, cells, stride=8), :] = vel_ref[axis]
    place[pl.ds(4 * 8 + 3, cells, stride=8), :] = kick_ref[...]
    tables = (left, right, moved)
    put_tables([pos_ref[axis] for axis in range(3)], occ_ref[...], tables, 4)
    steps = [(own, True, own < cells + 2) for own in range(4, cells + 3)]
    chain_forces(tables, weights, steps, add_kick(place, speed), GROUP)


def first_outer_kernel(
    cells, block_ref, edge_ref, occ_ref, kick_ref, place_ref, speed_ref, send_ref, info_ref,
    occ_all, kick_all, place, speed, weights, left, right, moved,
):
    half = cells // 4
    place[32:, :] = place_ref[32:, :]
    speed[32:, :] = speed_ref[32:, :]
    for axis in range(3):
        place[pl.ds(axis, 4, stride=8), :] = edge_ref[axis * 4 : axis * 4 + 4, :]
        speed[pl.ds(8 + axis, 3, stride=8), :] = edge_ref[12 + axis * 3 : 15 + axis * 3, :]
    place[pl.ds(8 + 3, 3, stride=8), :] = edge_ref[21:24, :]
    tables = (left, right, moved)
    planes = [place[pl.ds(axis, 8, stride=8), :] for axis in range(3)]
    occupied = jnp.concatenate([edge_ref[24:28, :], occ_ref[0:4, :]], axis=0)
    put_tables(planes, occupied, tables, 0)
    emit = add_kick(place, speed)
    carry = chain_forces(
        tables, weights, [(own, own > 0, True) for own in range(4)], emit, GROUP
    )
    emit(4, force_of(tables, 4, None, carry))
    occ_all[0:4, :] = edge_ref[24:28, :]
    occ_all[4 : cells + 4, :] = occ_ref[...]
    kick_all[0:3, :] = edge_ref[21:24, :]
    kick_all[3 : cells + 3, :] = kick_ref[...]
    start = 2 * block_ref[0] + 1
    for near in range(4):
        info_ref[near : near + 1, :] = occ_all[pl.ds(start + near, 1), :]
    for near in range(2):
        info_ref[4 + near : 5 + near, :] = kick_all[pl.ds(start + near, 1), :]
    info_ref[6:7, :] = occ_ref[0:1, :]
    info_ref[7:8, :] = jnp.zeros((1, LANES), F32)
    for kind, source in enumerate((place, speed)):
        for axis in range(3):
            for near in range(4):
                row = (kind * 3 + axis) * 4 + near
                for part in range(2):
                    first = (part * 2 * half + 1 + near) * 8 + axis
                    send_ref[pl.ds(part * WIDE + row, half, stride=2 * WIDE), :] = source[
                        pl.ds(first, half, stride=16), :
                    ]


def cycle(matrix, blocks):
    state = jnp.concatenate(blocks, axis=1)
    high = state.astype(BF16)
    low = (state - high.astype(F32)).astype(BF16)
    return jnp.dot(
        matrix, jnp.concatenate([high, low, high], axis=0), preferred_element_type=F32
    )


def lanes_of(array, index):
    return array[:, index * LANES : (index + 1) * LANES]


def middle_kernel(
    images, matrix_ref, info_ref, got_ref, send_ref, forces, weights, left, right, moved
):
    tables = (left, right, moved)

    def blocks_of(slots):
        return [
            jnp.concatenate(
                [
                    got_ref[pl.ds((kind * 3 + axis) * 4 + slot, images, stride=WIDE), :]
                    for kind in range(2)
                ],
                axis=0,
            )
            for slot in slots
            for axis in range(3)
        ]

    inner = cycle(matrix_ref[...], blocks_of((1, 2)))
    outer = cycle(matrix_ref[:images, :], blocks_of((0, 3)))
    for slot in range(4):
        source, first = ((outer, 0), (inner, 0), (inner, 3), (outer, 3))[slot]
        planes = [lanes_of(source, first + axis)[:images] for axis in range(3)]
        occupied = jnp.broadcast_to(info_ref[slot : slot + 1, :], (images, LANES))
        put_tables(planes, occupied, tables, slot * images, ("lr", "lrm", "lrm", "m")[slot])

    def emit(cell, force):
        row = (cell - images) * 8
        forces[row : row + 8, :] = force

    steps = [
        (slot * images + image, slot > 0, slot < 2)
        for image in range(images)
        for slot in range(3)
    ]
    chain_forces(tables, weights, steps, emit, 12, ahead=images)
    blocks = []
    for parity in range(2):
        kick = 2.0 * info_ref[4 + parity : 5 + parity, :]
        for axis in range(3):
            now = lanes_of(inner, parity * 3 + axis)
            force = forces[pl.ds(parity * images * 8 + axis, images, stride=8), :]
            blocks.append(jnp.concatenate([now[:images], now[images:] + kick * force], axis=0))
    ahead = cycle(matrix_ref[...], blocks)
    for parity in range(2):
        for axis in range(3):
            after = lanes_of(ahead, parity * 3 + axis)
            for kind in range(2):
                row = (kind * 3 + axis) * 2 + parity
                send_ref[pl.ds(row, images, stride=SPAN), :] = after[
                    kind * images : (kind + 1) * images
                ]


def last_inner_kernel(
    cells, got_ref, first_ref, occ_ref, kick_ref, place, speed,
    occ_all, weights, left, right, moved,
):
    half = cells // 4
    for kind, target in enumerate((place, speed)):
        for axis in range(3):
            for parity in range(2):
                row = (kind * 3 + axis) * 2 + parity
                for part in range(2):
                    first = (part * 2 * half + parity) * 8 + axis
                    target[pl.ds(first, half, stride=16), :] = got_ref[
                        pl.ds(part * SPAN + row, half, stride=2 * SPAN), :
                    ]
    place[pl.ds(2 * 8 + 3, cells, stride=8), :] = kick_ref[...]
    occ_all[0:2, :] = first_ref[26:28, :]
    occ_all[2:cells, :] = occ_ref[: cells - 2, :]
    tables = (left, right, moved)
    planes = [place[pl.ds(axis, cells, stride=8), :] for axis in range(3)]
    put_tables(planes, occ_all[...], tables, 0)
    emit = add_kick(place, speed)
    steps = [(own, own > 1, True) for own in range(1, cells - 1)]
    carry = chain_forces(tables, weights, steps, emit, GROUP)
    emit(cells - 1, force_of(tables, cells - 1, None, carry))


def last_outer_kernel(
    cells, edge_ref, occ_ref, place_ref, speed_ref, pos_ref, vel_ref,
    place, speed, weights, left, right, moved,
):
    base = cells - 8
    place[0:64, :] = place_ref[base * 8 : cells * 8, :]
    speed[0:64, :] = speed_ref[base * 8 : cells * 8, :]
    for axis in range(3):
        for parity in range(2):
            slot = (8 + parity) * 8 + axis
            row = axis * 2 + parity
            place[slot : slot + 1, :] = edge_ref[row : row + 1, :]
            speed[slot : slot + 1, :] = edge_ref[row + 6 : row + 7, :]
        slot = 10 * 8 + axis
        place[slot : slot + 1, :] = edge_ref[12 + axis : 13 + axis, :]
    for parity in range(2):
        slot = (8 + parity) * 8 + 3
        place[slot : slot + 1, :] = place_ref[
            (cells + parity) * 8 + 3 : (cells + parity) * 8 + 4, :
        ]
    tables = (left, right, moved)
    planes = [place[pl.ds(axis, 16, stride=8), :] for axis in range(3)]
    occupied = jnp.concatenate(
        [
            jnp.zeros((7, LANES), F32),
            occ_ref[cells - 3 : cells, :],
            edge_ref[15:16, :],
            jnp.zeros((5, LANES), F32),
        ],
        axis=0,
    )
    put_tables(planes, occupied, tables, 0)
    steps = [(own, True, own < 9) for own in range(7, 10)]
    chain_forces(tables, weights, steps, add_kick(place, speed), GROUP)
    for axis in range(3):
        for out_ref, whole, end in ((pos_ref, place_ref, place), (vel_ref, speed_ref, speed)):
            out_ref[axis, 0 : base, :] = whole[pl.ds(2 * 8 + axis, base, stride=8), :]
            out_ref[axis, base:cells, :] = end[pl.ds(2 * 8 + axis, 8, stride=8), :]


def local(positions, velocities, counts, types, masses):
    images = lax.axis_size("image")
    slabs = lax.axis_size("space")
    cells = positions.shape[1]
    rows = cells + 8

    def slab_shift(array, distance):
        pairs = [(s, (s + distance) % slabs) for s in range(slabs)]
        return lax.ppermute(array, "space", pairs)

    def transpose(array):
        blocks = array.reshape(images, array.shape[0] // images // 4, 4, LANES)
        blocks = lax.all_to_all(blocks, "image", split_axis=0, concat_axis=0, tiled=True)
        return blocks.reshape(array.shape)

    def call(kernel, outs, scratches, *args):
        return pl.pallas_call(
            kernel,
            out_shape=outs,
            in_specs=[SMEM if arg.ndim == 1 else VMEM for arg in args],
            out_specs=jax.tree.map(lambda _: VMEM, outs),
            scratch_shapes=scratches,
            compiler_params=PARAMS,
            cost_estimate=pl.CostEstimate(
                flops=20_000_000_000, bytes_accessed=1_000_000, transcendentals=0
            ),
        )(*args)

    def shaped(*shape):
        return jax.ShapeDtypeStruct(shape, F32)

    def weight_scratch(steps):
        return pltpu.VMEM((steps * LANES, 2 * LANES), BF16)

    slot_index = lax.broadcasted_iota(jnp.int32, types.shape, 1)
    occupied = (slot_index < counts[:, None]).astype(F32)
    type_index = lax.broadcasted_iota(jnp.int32, (masses.shape[0],) + types.shape, 0)
    chosen = jnp.sum(jnp.where(types[None] == type_index, masses[:, None, None], 0.0), axis=0)
    kick = 0.5 * time_step * (1.0 / chosen)
    matrix = jnp.asarray(cycle_matrix(images))
    group = lax.axis_index("image")
    block = (group % 2) * (images // 2) + group // 2

    pos = positions[0].transpose(1, 0, 2)
    vel = velocities[0].transpose(1, 0, 2)
    window = shaped(rows * 8, LANES)
    slab_scratch = [weight_scratch(cells)] + [scratch(rows * ROWS)] * 3
    edge_scratch = [scratch(rows * 8)] * 2 + [weight_scratch(8)] + [scratch(16 * ROWS)] * 3
    last = cells // 8 - 1
    edge = pl.pallas_call(
        lambda *r: edge_kernel(cells, *r),
        grid=(1,),
        out_shape=shaped(32, LANES),
        in_specs=[
            SMEM,
            SMEM,
            pl.BlockSpec((3, 8, LANES), lambda i: (0, last, 0)),
            pl.BlockSpec((3, 8, LANES), lambda i: (0, last, 0)),
            pl.BlockSpec((8, LANES), lambda i: (last, 0)),
        ],
        out_specs=pl.BlockSpec((32, LANES), lambda i: (0, 0)),
        compiler_params=pltpu.CompilerParams(vmem_limit_bytes=62 * 1024 * 1024),
    )(counts, masses, pos, vel, types)
    edge = slab_shift(edge, 1)
    place, speed = call(
        lambda *r: first_inner_kernel(cells, *r),
        (window, window),
        slab_scratch,
        pos, vel, occupied, kick,
    )
    send, info = call(
        lambda *r: first_outer_kernel(cells, *r),
        (shaped(images * WIDE, LANES), shaped(8, LANES)),
        [scratch(rows)] * 2 + edge_scratch,
        block.reshape(1), edge, occupied, kick, place, speed,
    )
    got = transpose(send)
    send = call(
        lambda *r: middle_kernel(images, *r),
        shaped(images * SPAN, LANES),
        [scratch(2 * images * 8), weight_scratch(3 * images)] + [scratch(4 * images * ROWS)] * 3,
        matrix, info, got,
    )
    got, info = lax.optimization_barrier((transpose(send), info))
    chunk = 2 * SPAN
    message = jnp.concatenate(
        [got[0:SPAN]]
        + [got[chunk + 2 * axis : chunk + 2 * axis + 1] for axis in range(3)]
        + [info[6:7]],
        axis=0,
    )
    message = slab_shift(message, -1)
    place, speed = call(
        lambda *r: last_inner_kernel(cells, *r),
        (window, window),
        [scratch(cells)] + slab_scratch,
        got, edge, occupied, kick,
    )
    pos, vel = call(
        lambda *r: last_outer_kernel(cells, *r),
        (shaped(*pos.shape), shaped(*vel.shape)),
        edge_scratch,
        message, occupied, place, speed,
    )
    return pos.transpose(1, 0, 2)[None], vel.transpose(1, 0, 2)[None]


def solution(mesh):
    return jax.shard_map(
        local,
        mesh=mesh,
        in_specs=(
            P("image", "space", None, None),
            P("image", "space", None, None),
            P("space"),
            P("space", None),
            P(),
        ),
        out_specs=(P("image", "space", None, None), P("image", "space", None, None)),
        check_vma=False,
    )
```
